256 devices in a mesh: member: 8 (over x_lo, y), space: 32 (over z, x_hi, core).
Axes of the slice: x: 4 (x_hi: 2, x_lo: 2; x = x_hi * 2 + x_lo), y: 4, z: 8, core: 2. Of those that a mesh axis runs over, the one named last changes fastest.
Arguments:
- features: bfloat16 [16, 32, 256, 1024], P('member', None, 'space'), may hold values from -6 to 6
- skip: bfloat16 [16, 32, 256, 1024], P('member', None, 'space'), may hold values from -6 to 6
- conv_weight: bfloat16 [3, 3, 32, 32], replicated, may hold values from -0.625 to 0.625
- out_weight: bfloat16 [2, 32], replicated, may hold values from -2 to 2
- target: float32 [2, 256, 1024], P(None, 'space'), may hold values from -12 to 12
Outputs:
- grad_input: bfloat16 [16, 32, 256, 1024], P('member', None, 'space')
The draws below stay inside these ranges and needn't reach their ends.
All inputs are finite; a program needn't handle non-finite values.
Results may differ from the reference program's by a relative error of at most 0.012.
Values may be sent and summed in bfloat16 or wider, within the bound.
No kernel may reach another device: no remote copies, remote signals or barrier semaphores. Data moves between devices by JAX's collectives and lax.ppermute only.
A program may use at most 64 MiB of HBM per device.

```python
import math
import jax
import jax.numpy as jnp
from jax import lax

C = 32
OUT = 2
COLS = 1024
MEMBERS = 16
ROWS = 256


def levels(stream_key, dims, cuts, smallest, top_value):
    def one(position, shards_of):
        steps = jax.random.uniform(jax.random.fold_in(jax.random.fold_in(stream_key, 6), position), (shards_of,), jnp.float32, smallest / len(cuts), top_value / len(cuts))
        return jnp.repeat(jnp.exp(steps), dims[position] // shards_of).reshape((-1,) + (1,) * (len(dims) - position - 1))

    gain = one(*cuts[0])
    for cut in cuts[1:]:
        gain = gain * one(*cut)
    return gain


def bell_draw(rng, dims, width, limit, split=(), dtype=jnp.bfloat16):
    values = width * jax.random.normal(rng, dims, jnp.float32)
    if split:
        values = values * levels(rng, dims, split, -0.22, 0.18)
    return jnp.clip(values, -limit, limit).astype(dtype)


def setup_inputs(seed: int = 0) -> dict:
    streams_of = jax.random.split(jax.random.key(seed), 6)
    features = bell_draw(streams_of[0], (MEMBERS, C, ROWS, COLS), 1.0, 6.0, ((0, 8), (2, 32)))
    skip = bell_draw(streams_of[1], (MEMBERS, C, ROWS, COLS), 1.0, 6.0, ((0, 8), (2, 32)))
    conv_weight = bell_draw(streams_of[2], (3, 3, C, C), (3 * C) ** -0.5, 0.625)
    out_weight = bell_draw(streams_of[3], (OUT, C), (C // 4) ** -0.5, 2.0)
    target = bell_draw(streams_of[4], (OUT, ROWS, COLS), 2.0, 12.0, ((1, 32),), jnp.float32)
    return dict(features=features, skip=skip, conv_weight=conv_weight, out_weight=out_weight, target=target)


root_coef = math.sqrt(2.0 / math.pi)
cubic_coef = 0.044715
smooth = 0.25

def gelu_value(source):
    inside = root_coef * (source + cubic_coef * source * source * source)
    return 0.5 * source * (1.0 + jnp.tanh(inside))

def gelu_slope(source):
    inside = root_coef * (source + cubic_coef * source * source * source)
    tanh_val = jnp.tanh(inside)
    return 0.5 * (1.0 + tanh_val) + 0.5 * source * (1.0 - tanh_val * tanh_val) * root_coef * (1.0 + 3.0 * cubic_coef * source * source)

def smooth_slope(source):
    return source / jnp.sqrt(source * source + smooth * smooth)

def stacked_taps(padded, row_count, col_count, flipped):
    pieces = []
    for row_tap in range(3):
        for col_tap in range(3):
            row_at = 2 - row_tap if flipped else row_tap
            col_at = 2 - col_tap if flipped else col_tap
            pieces.append(padded[:, row_at:row_at + row_count, col_at:col_at + col_count])
    return jnp.concatenate(pieces, axis=0).reshape(9 * padded.shape[0], row_count * col_count)

def conv_apply(source, weight, flipped):
    row_count, col_count = (source.shape[1], source.shape[2])
    padded = jnp.pad(source, ((0, 0), (1, 1), (1, 1)))
    if flipped:
        matrix = jnp.transpose(weight, (3, 0, 1, 2)).reshape(weight.shape[3], -1)
    else:
        matrix = jnp.transpose(weight, (2, 0, 1, 3)).reshape(weight.shape[2], -1)
    result = jnp.dot(matrix, stacked_taps(padded, row_count, col_count, flipped), preferred_element_type=jnp.float32)
    return result.reshape(matrix.shape[0], row_count, col_count)

def reference(features, skip, conv_weight, out_weight, target):
    member_total = features.shape[0]

    def forward_one(packed):
        source, bypass = packed
        preact = conv_apply(source, conv_weight, False) + bypass.astype(jnp.float32)
        active = gelu_value(preact).astype(jnp.bfloat16)
        flat = jnp.dot(out_weight, active.reshape(active.shape[0], -1), preferred_element_type=jnp.float32)
        return flat.reshape(out_weight.shape[0], active.shape[1], active.shape[2])
    outputs = lax.map(forward_one, (features, skip))

    def score_one(own_value):
        pair_term = lax.optimization_barrier(jnp.sum(smooth_slope(own_value[None] - outputs), axis=0))
        return smooth_slope(own_value - target) - pair_term / (member_total - 1)
    grad_out = lax.map(score_one, outputs).astype(jnp.bfloat16)

    def backward_one(triple):
        source, bypass, grad_member = triple
        preact = conv_apply(source, conv_weight, False) + bypass.astype(jnp.float32)
        flat = jnp.dot(out_weight.T, grad_member.reshape(grad_member.shape[0], -1), preferred_element_type=jnp.float32)
        grad_active = flat.reshape(preact.shape)
        grad_preact = (grad_active * gelu_slope(preact)).astype(jnp.bfloat16)
        return conv_apply(grad_preact, conv_weight, True).astype(jnp.bfloat16)
    return lax.map(backward_one, (features, skip, grad_out))
```

```python
import functools
import math

import jax
import jax.numpy as jnp
from jax import lax
from jax.experimental import pallas as pl
from jax.experimental.pallas import tpu as pltpu
from jax.sharding import PartitionSpec as P

root_coef = math.sqrt(2.0 / math.pi)
cubic_coef = 0.044715
smooth = 0.25

CH = 32
RW = 8
W = 1024
FULL = CH * RW
EDGE = 4 * CH
PK = 96
PKT = 2 * PK + 16
bf16, f32 = jnp.bfloat16, jnp.float32


def iota(shape, dim):
    return lax.broadcasted_iota(jnp.int32, shape, dim)


def dot(a, b):
    return jnp.dot(a, b, preferred_element_type=f32)


def dot_nt(a, b):
    return lax.dot_general(a, b, (((1,), (1,)), ((), ())), preferred_element_type=f32)


def mod(a, n):
    return jnp.bitwise_and(a, n - 1)


def div(a, n):
    return lax.shift_right_logical(a, int(math.log2(n)))


def edge_row(e):
    return jnp.where(e < 2, e - 1, e + 5)


def halo_row(q):
    return jnp.where(q < 4, q - 2, q + 2)


def moved(x, step):
    zero = jnp.zeros((x.shape[0], 1), x.dtype)
    if step == 1:
        return jnp.concatenate([x[:, 1:], zero], axis=1)
    if step == -1:
        return jnp.concatenate([zero, x[:, :-1]], axis=1)
    return x


def gelu_pair(v):
    u = v * v
    h = 0.5 + 0.5 * jnp.tanh(v * (root_coef + (root_coef * cubic_coef) * u))
    slope = h + (v * (h - h * h)) * (2.0 * root_coef + (6.0 * root_coef * cubic_coef) * u)
    return v * h, slope


def smooth_slope(u):
    return u * lax.rsqrt(u * u + smooth * smooth)


def pack_kernel(feat, skip, target, up, down):
    r, c = iota((EDGE, FULL), 0), iota((EDGE, FULL), 1)
    q = div(r, CH)
    row = jnp.where(q < 2, q, q + 4)
    pick = ((div(c, RW) == mod(r, CH)) & (mod(c, RW) == row)).astype(f32).astype(bf16)
    r2, c2 = iota((2 * CH, FULL), 0), iota((2 * CH, FULL), 1)
    pick2 = ((div(c2, RW) == mod(r2, CH)) & (mod(c2, RW) == jnp.where(r2 < CH, 0, 7))).astype(f32).astype(bf16)
    for m in range(2):
        rows = dot(pick, feat[m]).astype(bf16)
        up[m * PK : m * PK + 64] = rows[:64]
        down[m * PK : m * PK + 64] = rows[64:]
        rows = dot(pick2, skip[m]).astype(bf16)
        up[m * PK + 64 : m * PK + 96] = rows[:32]
        down[m * PK + 64 : m * PK + 96] = rows[32:]
    line = iota((16, W), 0)
    for out, at in ((up, 0), (down, 7)):
        left = [target[at : at + 1, :], target[8 + at : 9 + at, :]]
        total = jnp.zeros((16, W), f32)
        for term in range(3):
            for k in range(2):
                part = left[k].astype(bf16).astype(f32)
                left[k] = left[k] - part
                total = jnp.where(line == 2 * term + k, part, total)
        out[2 * PK : PKT] = total.astype(bf16)


def mats_kernel(weight, out_weight, b_main, b_edge, b_back, p_main, p_edge, spread):
    place = lax.axis_index("space")
    ro = (div(iota((FULL, CH), 0), RW) == iota((FULL, CH), 1)).astype(f32).astype(bf16)
    re = (mod(iota((EDGE, CH), 0), CH) == iota((EDGE, CH), 1)).astype(f32).astype(bf16)
    rq = (mod(iota((FULL, CH), 0), CH) == iota((FULL, CH), 1)).astype(f32).astype(bf16)
    r, c = iota((FULL, FULL), 0), iota((FULL, FULL), 1)
    row_of, row_at = mod(r, RW), mod(c, RW)
    inner = (row_at > 0) & (row_at < RW - 1)
    er, ec = iota((EDGE, FULL), 0), iota((EDGE, FULL), 1)
    step_edge = halo_row(div(ec, CH)) - edge_row(div(er, CH))
    br, bc = iota((FULL, EDGE), 0), iota((FULL, EDGE), 1)
    step_back = mod(br, RW) - edge_row(div(bc, CH))
    for d in range(3):
        main = jnp.zeros((FULL, FULL), f32)
        edge = jnp.zeros((EDGE, FULL), f32)
        back = jnp.zeros((FULL, FULL), f32)
        back_edge = jnp.zeros((FULL, EDGE), f32)
        for a in range(3):
            w = weight[a * 3 + d]
            main = jnp.where(row_at - row_of == a - 1, dot_nt(dot(ro, w).astype(bf16), ro), main)
            edge = jnp.where(step_edge == a - 1, dot_nt(dot(re, w).astype(bf16), rq), edge)
            t = dot_nt(ro, w).astype(bf16)
            back = jnp.where((row_of - row_at == a - 1) & inner, dot_nt(t, ro), back)
            back_edge = jnp.where(step_back == a - 1, dot_nt(t, re), back_edge)
        b_main[:, d * FULL : (d + 1) * FULL] = main.astype(bf16)
        b_edge[:, d * FULL : (d + 1) * FULL] = edge.astype(bf16)
        at = d * (FULL + EDGE)
        b_back[:, at : at + FULL] = back.astype(bf16)
        b_back[:, at + FULL : at + FULL + EDGE] = back_edge.astype(bf16)

    ow = out_weight[...].astype(f32)
    line = iota((32, CH), 0)
    second = jnp.where(line < 16, div(line, 8), mod(div(line, 2), 2)) == 1
    rows_w = jnp.where(second, ow[1:2, :], ow[0:1, :]).astype(bf16)
    pr, pc = iota((16, FULL), 0), iota((16, FULL), 1)
    same = (mod(pr, RW) == mod(pc, RW)) & (mod(pr, RW) > 0) & (mod(pr, RW) < RW - 1)
    p_main[...] = jnp.where(same, dot_nt(rows_w[:16], ro), 0.0).astype(bf16)

    def edge_match(line, e, m):
        inside = (line < 16) & (mod(line, 8) == edge_row(e))
        outer = (div(line, 4) == 4 + m) & (e == jnp.where(mod(line, 2) == 0, 0, 3))
        return inside | outer

    lr, lc = iota((32, EDGE), 0), iota((32, EDGE), 1)
    wide = dot_nt(rows_w, re)
    for m in range(2):
        p_edge[m] = jnp.where(edge_match(lr, div(lc, CH), m), wide, 0.0).astype(bf16)
    sr, sc = iota((FULL, 32), 0), iota((FULL, 32), 1)
    whole = jnp.where((sc < 16) & (mod(sc, 8) == mod(sr, RW)), dot_nt(ro, rows_w), 0.0).astype(bf16)
    tr, tc = iota((EDGE, 32), 0), iota((EDGE, 32), 1)
    e = div(tr, CH)
    off = ((e == 0) & (place == 0)) | ((e == 3) & (place == lax.axis_size("space") - 1))
    tall = dot_nt(re, rows_w)
    for m in range(2):
        spread[m, :FULL] = whole
        spread[m, FULL:] = jnp.where(edge_match(tc, e, m) & ~off, tall, 0.0).astype(bf16)


def main_kernel(feat, skip, b_main, p_main, slope, part, taps, pre, act):
    for m in range(2):
        x = feat[m]
        for d in range(3):
            taps[d * FULL : (d + 1) * FULL] = moved(x, d - 1)
        pre[...] = dot(b_main[...], taps[...])

        def rows(i, _):
            at = pl.ds(pl.multiple_of(i * 16, 16), 16)
            for half in range(2):
                cols = slice(half * 512, half * 512 + 512)
                a, s = gelu_pair(pre[at, cols] + skip[m, at, cols].astype(f32))
                act[at, cols] = a.astype(bf16)
                slope[m, at, cols] = s
            return 0

        lax.fori_loop(0, FULL // 16, rows, 0)
        part[m] = dot(p_main[...], act[...])


def edge_kernel(above, below, up, down, b_edge, p_edge, part, slope, own, send, halo_target, taps, pre, act):
    halo = jnp.zeros((8, W), f32)
    for m in range(2):
        at = m * PK
        x = jnp.concatenate(
            [above[at : at + 64], up[at : at + 64], down[at : at + 64], below[at : at + 64]], axis=0
        )
        for d in range(3):
            taps[d * FULL : (d + 1) * FULL] = moved(x, d - 1)
        pre[...] = dot(b_edge[...], taps[...])
        for e, source in enumerate((above, up, down, below)):
            for part_at in range(2):
                rows = slice(e * CH + part_at * 16, e * CH + part_at * 16 + 16)
                from_rows = slice(at + 64 + part_at * 16, at + 80 + part_at * 16)
                for half in range(2):
                    cols = slice(half * 512, half * 512 + 512)
                    a, s = gelu_pair(pre[rows, cols] + source[from_rows, cols].astype(f32))
                    act[rows, cols] = a.astype(bf16)
                    slope[m, rows, cols] = s
        more = dot(p_edge[m], act[...])
        own[m * 16 : m * 16 + 16] = part[m] + more[:16]
        halo = halo + more[16:24]
    own[32:40] = halo
    both = jnp.concatenate([own[:, :512], own[:, 512:]], axis=0).astype(bf16)
    for k in range(8):
        send[k] = both
    line = iota((8, W), 0)
    total = jnp.zeros((8, W), f32)
    for h, source in enumerate((above, below)):
        terms = source[2 * PK : PKT].astype(f32)
        for k in range(2):
            value = (terms[k : k + 1] + terms[2 + k : 3 + k]) + terms[4 + k : 5 + k]
            total = jnp.where(mod(line, 4) == 2 * k + h, value, total)
    halo_target[...] = total


def back_kernel(got, own, target, halo_target, slope, slope_edge, spread, b_back, out, grad, ga, taps):
    me = lax.axis_index("member")
    grad[...] = jnp.zeros(grad.shape, bf16)
    width = 256
    for c in range(512 // width):
        here = [slice(h * 512 + c * width, h * 512 + (c + 1) * width) for h in range(2)]
        mine, sums = [], []
        for h in range(2):
            o0, o1, oh = own[0:16, here[h]], own[16:32, here[h]], own[32:40, here[h]]
            t = smooth_slope(o0 - o1)
            mine.append((o0, o1, oh))
            sums.append([t, -t, smooth_slope(oh - jnp.concatenate([oh[4:], oh[:4]], axis=0))])
        for j in range(1, 8):
            theirs = got[mod(me + j, 8), :, c * width : (c + 1) * width].astype(f32)
            for h in range(2):
                o0, o1, oh = mine[h]
                x = theirs[40 * h : 40 * h + 40]
                x0, x1, xh = x[0:16], x[16:32], x[32:40]
                sums[h][0] += smooth_slope(o0 - x0) + smooth_slope(o0 - x1)
                sums[h][1] += smooth_slope(o1 - x0) + smooth_slope(o1 - x1)
                swapped = jnp.concatenate([xh[4:], xh[:4]], axis=0)
                sums[h][2] += smooth_slope(oh - xh) + smooth_slope(oh - swapped)
        for h in range(2):
            o0, o1, oh = mine[h]
            t = target[:, here[h]]
            gh = smooth_slope(oh - halo_target[:, here[h]]) - sums[h][2] * (1.0 / 15.0)
            tail = jnp.concatenate([gh, jnp.zeros_like(gh)], axis=0).astype(bf16)
            for m, o in enumerate((o0, o1)):
                grad[m, 0:16, here[h]] = (smooth_slope(o - t) - sums[h][m] * (1.0 / 15.0)).astype(bf16)
                grad[m, 16:32, here[h]] = tail
    size = FULL + EDGE
    for m in range(2):
        ga[...] = dot(spread[m], grad[m])

        def rows(i, _):
            at = pl.ds(pl.multiple_of(i * 16, 16), 16)
            taps[pl.ds(pl.multiple_of(size + i * 16, 16), 16), :] = (ga[at, :] * slope[m, at, :]).astype(bf16)
            return 0

        lax.fori_loop(0, FULL // 16, rows, 0)
        for i in range(EDGE // 16):
            at = FULL + i * 16
            taps[size + at : size + at + 16] = (ga[at : at + 16] * slope_edge[m, i * 16 : i * 16 + 16]).astype(bf16)
        g = taps[size : 2 * size]
        taps[0:size] = moved(g, 1)
        taps[2 * size : 3 * size] = moved(g, -1)
        out[m] = dot(b_back[...], taps[...]).astype(bf16)


def call(kernel, outs, scratch, flops, *args):
    return pl.pallas_call(
        kernel,
        out_shape=outs,
        in_specs=[pl.BlockSpec(memory_space=pltpu.VMEM)] * len(args),
        out_specs=[pl.BlockSpec(memory_space=pltpu.VMEM)] * len(outs),
        scratch_shapes=scratch,
        compiler_params=pltpu.CompilerParams(vmem_limit_bytes=32 * 1024 * 1024),
        cost_estimate=pl.CostEstimate(flops=flops, bytes_accessed=1 << 20, transcendentals=0),
    )(*args)


def local(features, skip, conv_weight, out_weight, target):
    S = jax.ShapeDtypeStruct
    V = pltpu.VMEM
    feat = features.reshape(2, FULL, W)
    bypass = skip.reshape(2, FULL, W)
    goal = target.reshape(16, W)
    up, down = call(pack_kernel, [S((PKT, W), bf16)] * 2, [], 1 << 29, feat, bypass, goal)
    count = lax.axis_size("space")
    above = lax.ppermute(down, "space", [(i, i + 1) for i in range(count - 1)])
    below = lax.ppermute(up, "space", [(i + 1, i) for i in range(count - 1)])
    b_main, b_edge, b_back, p_main, p_edge, spread = call(
        mats_kernel,
        [
            S((FULL, 3 * FULL), bf16),
            S((EDGE, 3 * FULL), bf16),
            S((FULL, 3 * (FULL + EDGE)), bf16),
            S((16, FULL), bf16),
            S((2, 32, EDGE), bf16),
            S((2, FULL + EDGE, 32), bf16),
        ],
        [],
        1 << 31,
        conv_weight.reshape(9, CH, CH),
        out_weight,
    )
    slope, part = call(
        main_kernel,
        [S((2, FULL, W), f32), S((2, 16, W), f32)],
        [V((3 * FULL, W), bf16), V((FULL, W), f32), V((FULL, W), bf16)],
        1 << 31,
        feat,
        bypass,
        b_main,
        p_main,
    )
    slope_edge, own, send, halo_target = call(
        edge_kernel,
        [S((2, EDGE, W), f32), S((40, W), f32), S((8, 80, 512), bf16), S((8, W), f32)],
        [V((3 * FULL, W), bf16), V((EDGE, W), f32), V((EDGE, W), bf16)],
        1 << 30,
        above,
        below,
        up,
        down,
        b_edge,
        p_edge,
        part,
    )
    got = lax.all_to_all(send, "member", split_axis=0, concat_axis=0, tiled=True)
    size = FULL + EDGE
    (out,) = call(
        back_kernel,
        [S((2, FULL, W), bf16)],
        [V((2, 32, W), bf16), V((size, W), f32), V((3 * size, W), bf16)],
        1 << 31,
        got,
        own,
        goal,
        halo_target,
        slope,
        slope_edge,
        spread,
        b_back,
    )
    return out.reshape(2, CH, RW, W)


def solution(mesh):
    placed = (
        P("member", None, "space", None),
        P("member", None, "space", None),
        P(),
        P(),
        P(None, "space", None),
    )
    return jax.shard_map(
        local,
        mesh=mesh,
        in_specs=placed,
        out_specs=P("member", None, "space", None),
        check_vma=False,
    )
```

```python
import functools
import math

import jax
import jax.numpy as jnp
from jax import lax
from jax.experimental import pallas as pl
from jax.experimental.pallas import tpu as pltpu
from jax.sharding import PartitionSpec as P

root_coef = math.sqrt(2.0 / math.pi)
cubic_coef = 0.044715
smooth = 0.25

CH = 32
RW = 8
W = 1024
FULL = CH * RW
EDGE = 4 * CH
PK = 64
PKT = 2 * PK + 8
bf16, f32 = jnp.bfloat16, jnp.float32


def iota(shape, dim):
    return lax.broadcasted_iota(jnp.int32, shape, dim)


def dot(a, b):
    return jnp.dot(a, b, preferred_element_type=f32)


def dot_nt(a, b):
    return lax.dot_general(a, b, (((1,), (1,)), ((), ())), preferred_element_type=f32)


def mod(a, n):
    return jnp.bitwise_and(a, n - 1)


def div(a, n):
    return lax.shift_right_logical(a, int(math.log2(n)))


def edge_row(e, odd):
    row = jnp.where(e < 2, e - 1, e + 5)
    return jnp.where(odd, 7 - row, row)


def facing(x):
    return jnp.bitwise_xor(x, 1)


def moved(x, step):
    zero = jnp.zeros((x.shape[0], 1), x.dtype)
    if step == 1:
        return jnp.concatenate([x[:, 1:], zero], axis=1)
    if step == -1:
        return jnp.concatenate([zero, x[:, :-1]], axis=1)
    return x


def gelu_pair(v):
    u = v * v
    h = 0.5 + 0.5 * jnp.tanh(v * (root_coef + (root_coef * cubic_coef) * u))
    slope = h + (v * (h - h * h)) * (2.0 * root_coef + (6.0 * root_coef * cubic_coef) * u)
    return v * h, slope


def smooth_slope(u):
    return u * lax.rsqrt(u * u + smooth * smooth)


def edge_rows(odd, weight):
    r, c = iota((EDGE, FULL), 0), iota((EDGE, FULL), 1)
    q = div(r, CH)
    top = (q < 2) != odd
    row = jnp.where(top, mod(q, 2), 7 - mod(q, 2))
    pick = ((div(c, RW) == mod(r, CH)) & (mod(c, RW) == row)).astype(f32).astype(bf16)
    r2, c2 = iota((2 * CH, FULL), 0), iota((2 * CH, FULL), 1)
    row = edge_row(1 + div(r2, CH), odd)
    pick2 = ((div(c2, RW) == mod(r2, CH)) & (mod(c2, RW) == row)).astype(f32).astype(bf16)
    blocks, none = [], jnp.zeros((CH, 2 * CH), f32)
    for d in range(3):
        low, mid, high = (weight[a * 3 + d].astype(f32) for a in range(3))
        one = jnp.concatenate([mid, jnp.where(odd, low, high), none], axis=1)
        two = jnp.concatenate([none, mid, jnp.where(odd, high, low)], axis=1)
        blocks.append(jnp.concatenate([one, two], axis=0))
    lend = jnp.concatenate(blocks, axis=1).astype(bf16)

    def rows(feat, skip):
        x = dot(pick, feat).astype(bf16)
        taps = jnp.concatenate([moved(x, d - 1) for d in range(3)], axis=0)
        return x, dot(lend, taps) + dot(pick2, skip)

    return rows


def pack_kernel(feat_in, skip_in, target_in, weight_in, across, beside, feat, skip, target, weight, one, two, sems):
    copies = [pltpu.make_async_copy(target_in, target, sems.at[4]), pltpu.make_async_copy(weight_in, weight, sems.at[5])]
    for m in range(2):
        copies.append(pltpu.make_async_copy(feat_in.at[m], feat.at[m], sems.at[m]))
        copies.append(pltpu.make_async_copy(skip_in.at[m], skip.at[m], sems.at[2 + m]))
    for copy in copies:
        copy.start()
    odd = mod(lax.axis_index("space"), 2) == 1
    copies[0].wait()
    copies[1].wait()
    line = iota((8, W), 0)
    for out, at, other in ((one, 0, 7), (two, 7, 0)):
        left = [jnp.where(odd, target[k + other : k + other + 1, :], target[k + at : k + at + 1, :]) for k in (0, 8)]
        total = jnp.zeros((8, W), f32)
        for term in range(3):
            for k in range(2):
                part = left[k].astype(bf16).astype(f32)
                left[k] = left[k] - part
                total = jnp.where(line == 2 * term + k, part, total)
        out[2 * PK : PKT] = total.astype(bf16)
    rows = edge_rows(odd, weight)
    for m in range(2):
        copies[2 + 2 * m].wait()
        copies[3 + 2 * m].wait()
        x, part = rows(feat[m], skip[m])
        part = part.astype(bf16)
        one[m * PK : m * PK + 32] = x[0:32]
        two[m * PK : m * PK + 32] = x[64:96]
        one[m * PK + 32 : m * PK + 64] = part[:32]
        two[m * PK + 32 : m * PK + 64] = part[32:]
    last = [pltpu.make_async_copy(one, across, sems.at[6]), pltpu.make_async_copy(two, beside, sems.at[7])]
    for copy in last:
        copy.start()
    for copy in last:
        copy.wait()


def mats_kernel(weight, out_weight, b_main, b_edge, b_back, p_main, p_edge, spread):
    place = lax.axis_index("space")
    odd = mod(place, 2) == 1
    ro = (div(iota((FULL, CH), 0), RW) == iota((FULL, CH), 1)).astype(f32).astype(bf16)
    re = (mod(iota((EDGE, CH), 0), CH) == iota((EDGE, CH), 1)).astype(f32).astype(bf16)
    r, c = iota((FULL, FULL), 0), iota((FULL, FULL), 1)
    row_of, row_at = mod(r, RW), mod(c, RW)
    inner = (row_at > 0) & (row_at < RW - 1)
    er, ec = div(iota((EDGE, EDGE), 0), CH), div(iota((EDGE, EDGE), 1), CH)
    step_edge = jnp.where(er == ec, edge_row(facing(er), odd) - edge_row(er, odd), 9)
    br, bc = iota((FULL, EDGE), 0), iota((FULL, EDGE), 1)
    step_back = mod(br, RW) - edge_row(div(bc, CH), odd)
    for d in range(3):
        main = jnp.zeros((FULL, FULL), f32)
        edge = jnp.zeros((EDGE, EDGE), f32)
        back = jnp.zeros((FULL, FULL), f32)
        back_edge = jnp.zeros((FULL, EDGE), f32)
        for a in range(3):
            w = weight[a * 3 + d]
            main = jnp.where(row_at - row_of == a - 1, dot_nt(dot(ro, w).astype(bf16), ro), main)
            edge = jnp.where(step_edge == a - 1, dot_nt(dot(re, w).astype(bf16), re), edge)
            t = dot_nt(ro, w).astype(bf16)
            back = jnp.where((row_of - row_at == a - 1) & inner, dot_nt(t, ro), back)
            back_edge = jnp.where(step_back == a - 1, dot_nt(t, re), back_edge)
        b_main[:, d * FULL : (d + 1) * FULL] = main.astype(bf16)
        b_edge[:, d * EDGE : (d + 1) * EDGE] = edge.astype(bf16)
        at = d * (FULL + EDGE)
        b_back[:, at : at + FULL] = back.astype(bf16)
        b_back[:, at + FULL : at + FULL + EDGE] = back_edge.astype(bf16)

    ow = out_weight[...].astype(f32)
    line = iota((32, CH), 0)
    second = jnp.where(line < 16, div(line, 8), mod(div(line, 2), 2)) == 1
    rows_w = jnp.where(second, ow[1:2, :], ow[0:1, :]).astype(bf16)
    pr, pc = iota((16, FULL), 0), iota((16, FULL), 1)
    same = (mod(pr, RW) == mod(pc, RW)) & (mod(pr, RW) > 0) & (mod(pr, RW) < RW - 1)
    p_main[...] = jnp.where(same, dot_nt(rows_w[:16], ro), 0.0).astype(bf16)

    def edge_match(line, e, m):
        inside = (line < 16) & (mod(line, 8) == edge_row(e, odd))
        outer = (div(line, 4) == 4 + m) & (e == jnp.where(mod(line, 2) == 0, 0, 3))
        return inside | outer

    lr, lc = iota((32, EDGE), 0), iota((32, EDGE), 1)
    wide = dot_nt(rows_w, re)
    for m in range(2):
        p_edge[m] = jnp.where(edge_match(lr, div(lc, CH), m), wide, 0.0).astype(bf16)
    sr, sc = iota((FULL, 32), 0), iota((FULL, 32), 1)
    whole = jnp.where((sc < 16) & (mod(sc, 8) == mod(sr, RW)), dot_nt(ro, rows_w), 0.0).astype(bf16)
    tr, tc = iota((EDGE, 32), 0), iota((EDGE, 32), 1)
    e = div(tr, CH)
    off = (e == 0) & ((place == 0) | (place == lax.axis_size("space") - 1))
    tall = dot_nt(re, rows_w)
    for m in range(2):
        spread[m, :FULL] = whole
        spread[m, FULL:] = jnp.where(edge_match(tc, e, m) & ~off, tall, 0.0).astype(bf16)


def main_kernel(feat, skip, weight, b_main, p_main, slope, part, lent, taps, pre, act):
    edges = edge_rows(mod(lax.axis_index("space"), 2) == 1, weight)
    for m in range(2):
        x = feat[m]
        for d in range(3):
            taps[d * FULL : (d + 1) * FULL] = moved(x, d - 1)
        pre[...] = dot(b_main[...], taps[...])

        def rows(i, _):
            at = pl.ds(pl.multiple_of(i * 16, 16), 16)
            for half in range(2):
                cols = slice(half * 512, half * 512 + 512)
                a, s = gelu_pair(pre[at, cols] + skip[m, at, cols].astype(f32))
                act[at, cols] = a.astype(bf16)
                slope[m, at, cols] = s
            return 0

        lax.fori_loop(0, FULL // 16, rows, 0)
        part[m] = dot(p_main[...], act[...])
        lent[m] = edges(x, skip[m])[1]


def edge_kernel(got_across, got_beside, across, beside, b_edge, p_edge, part, lent, slope, own, send, halo_target, taps, pre, act):
    halo = jnp.zeros((8, W), f32)
    for m in range(2):
        at = m * PK
        x = jnp.concatenate(
            [across[at : at + 32], got_across[at : at + 32], got_beside[at : at + 32], beside[at : at + 32]], axis=0
        )
        for d in range(3):
            taps[d * EDGE : (d + 1) * EDGE] = moved(x, d - 1)
        pre[...] = dot(b_edge[...], taps[...])
        for e in range(4):
            for step in range(2):
                rows = slice(e * CH + step * 16, e * CH + step * 16 + 16)
                far = slice(at + 32 + step * 16, at + 48 + step * 16)
                near = slice((e - 1) * CH + step * 16, (e - 1) * CH + step * 16 + 16)
                for half in range(2):
                    cols = slice(half * 512, half * 512 + 512)
                    if e in (1, 2):
                        base = lent[m, near, cols]
                    else:
                        base = (got_beside if e else got_across)[far, cols].astype(f32)
                    a, s = gelu_pair(pre[rows, cols] + base)
                    act[rows, cols] = a.astype(bf16)
                    slope[m, rows, cols] = s
        more = dot(p_edge[m], act[...])
        own[m * 16 : m * 16 + 16] = part[m] + more[:16]
        halo = halo + more[16:24]
    own[32:40] = halo
    both = jnp.concatenate([own[:, :512], own[:, 512:]], axis=0).astype(bf16)
    for k in range(8):
        send[k] = both
    line = iota((8, W), 0)
    total = jnp.zeros((8, W), f32)
    for h, source in enumerate((got_across, got_beside)):
        terms = source[2 * PK : PKT].astype(f32)
        for k in range(2):
            value = (terms[k : k + 1] + terms[2 + k : 3 + k]) + terms[4 + k : 5 + k]
            total = jnp.where(mod(line, 4) == 2 * k + h, value, total)
    halo_target[...] = total


def back_kernel(got, own, target, halo_target, slope, slope_edge, spread, b_back, out, grad, ga, taps, ready, sems):
    me = lax.axis_index("member")
    grad[...] = jnp.zeros(grad.shape, bf16)
    width = 256
    for c in range(512 // width):
        here = [slice(h * 512 + c * width, h * 512 + (c + 1) * width) for h in range(2)]
        mine, sums = [], []
        for h in range(2):
            o0, o1, oh = own[0:16, here[h]], own[16:32, here[h]], own[32:40, here[h]]
            t = smooth_slope(o0 - o1)
            mine.append((o0, o1, oh))
            sums.append([t, -t, smooth_slope(oh - jnp.concatenate([oh[4:], oh[:4]], axis=0))])
        for j in range(1, 8):
            theirs = got[mod(me + j, 8), :, c * width : (c + 1) * width].astype(f32)
            for h in range(2):
                o0, o1, oh = mine[h]
                x = theirs[40 * h : 40 * h + 40]
                x0, x1, xh = x[0:16], x[16:32], x[32:40]
                sums[h][0] += smooth_slope(o0 - x0) + smooth_slope(o0 - x1)
                sums[h][1] += smooth_slope(o1 - x0) + smooth_slope(o1 - x1)
                swapped = jnp.concatenate([xh[4:], xh[:4]], axis=0)
                sums[h][2] += smooth_slope(oh - xh) + smooth_slope(oh - swapped)
        for h in range(2):
            o0, o1, oh = mine[h]
            t = target[:, here[h]]
            gh = smooth_slope(oh - halo_target[:, here[h]]) - sums[h][2] * (1.0 / 15.0)
            tail = jnp.concatenate([gh, jnp.zeros_like(gh)], axis=0).astype(bf16)
            for m, o in enumerate((o0, o1)):
                grad[m, 0:16, here[h]] = (smooth_slope(o - t) - sums[h][m] * (1.0 / 15.0)).astype(bf16)
                grad[m, 16:32, here[h]] = tail
    size = FULL + EDGE
    copies = []
    for m in range(2):
        ga[m] = dot(spread[m], grad[m])
        for i in range(FULL // 16):
            at = slice(i * 16, i * 16 + 16)
            taps[m, size + i * 16 : size + i * 16 + 16] = (ga[m, at] * slope[m, at]).astype(bf16)
        for i in range(EDGE // 16):
            at = FULL + i * 16
            taps[m, size + at : size + at + 16] = (ga[m, at : at + 16] * slope_edge[m, i * 16 : i * 16 + 16]).astype(bf16)
        g = taps[m, size : 2 * size]
        taps[m, 0:size] = moved(g, 1)
        taps[m, 2 * size : 3 * size] = moved(g, -1)
    for m in range(2):
        for h in range(2):
            cols = slice(h * 512, h * 512 + 512)
            ready[m, :, cols] = dot(b_back[...], taps[m, :, cols]).astype(bf16)
            copy = pltpu.make_async_copy(ready.at[m, :, cols], out.at[m, :, cols], sems.at[2 * m + h])
            copy.start()
            copies.append(copy)
    for copy in copies:
        copy.wait()


def call(kernel, outs, scratch, flops, *args, far=(), far_out=False, grant=32):
    near = pl.BlockSpec(memory_space=pltpu.VMEM)
    hbm = pl.BlockSpec(memory_space=pltpu.HBM)
    return pl.pallas_call(
        kernel,
        out_shape=outs,
        in_specs=[hbm if i in far else near for i in range(len(args))],
        out_specs=[hbm if far_out else near] * len(outs),
        scratch_shapes=scratch,
        compiler_params=pltpu.CompilerParams(vmem_limit_bytes=grant * 1024 * 1024),
        cost_estimate=pl.CostEstimate(flops=flops, bytes_accessed=1 << 20, transcendentals=0),
    )(*args)


def local(features, skip, conv_weight, out_weight, target):
    S = jax.ShapeDtypeStruct
    V = pltpu.VMEM
    feat = features.reshape(2, FULL, W)
    bypass = skip.reshape(2, FULL, W)
    goal = target.reshape(16, W)
    weight = conv_weight.reshape(9, CH, CH)
    dma = pltpu.SemaphoreType.DMA
    across, beside = call(
        pack_kernel,
        [S((PKT, W), bf16)] * 2,
        [
            V((2, FULL, W), bf16),
            V((2, FULL, W), bf16),
            V((16, W), f32),
            V((9, CH, CH), bf16),
            V((PKT, W), bf16),
            V((PKT, W), bf16),
            dma((8,)),
        ],
        1 << 29,
        feat,
        bypass,
        goal,
        weight,
        far=(0, 1, 2, 3),
        far_out=True,
        grant=60,
    )
    count = lax.axis_size("space")
    got_across = lax.ppermute(across, "space", [(i, ((i + 1) ^ 1) - 1) for i in range(1, count - 1)])
    got_beside = lax.ppermute(beside, "space", [(i, i ^ 1) for i in range(count)])
    b_main, b_edge, b_back, p_main, p_edge, spread = call(
        mats_kernel,
        [
            S((FULL, 3 * FULL), bf16),
            S((EDGE, 3 * EDGE), bf16),
            S((FULL, 3 * (FULL + EDGE)), bf16),
            S((16, FULL), bf16),
            S((2, 32, EDGE), bf16),
            S((2, FULL + EDGE, 32), bf16),
        ],
        [],
        1 << 31,
        weight,
        out_weight,
    )
    slope, part, lent = call(
        main_kernel,
        [S((2, FULL, W), f32), S((2, 16, W), f32), S((2, 2 * CH, W), f32)],
        [V((3 * FULL, W), bf16), V((FULL, W), f32), V((FULL, W), bf16)],
        1 << 31,
        feat,
        bypass,
        weight,
        b_main,
        p_main,
    )
    slope_edge, own, send, halo_target = call(
        edge_kernel,
        [S((2, EDGE, W), f32), S((40, W), f32), S((8, 80, 512), bf16), S((8, W), f32)],
        [V((3 * EDGE, W), bf16), V((EDGE, W), f32), V((EDGE, W), bf16)],
        1 << 30,
        got_across,
        got_beside,
        across,
        beside,
        b_edge,
        p_edge,
        part,
        lent,
    )
    got = lax.all_to_all(send, "member", split_axis=0, concat_axis=0, tiled=True)
    size = FULL + EDGE
    (out,) = call(
        back_kernel,
        [S((2, FULL, W), bf16)],
        [
            V((2, 32, W), bf16),
            V((2, size, W), f32),
            V((2, 3 * size, W), bf16),
            V((2, FULL, W), bf16),
            dma((4,)),
        ],
        1 << 31,
        got,
        own,
        goal,
        halo_target,
        slope,
        slope_edge,
        spread,
        b_back,
        far_out=True,
    )
    return out.reshape(2, CH, RW, W)


def solution(mesh):
    placed = (
        P("member", None, "space", None),
        P("member", None, "space", None),
        P(),
        P(),
        P(None, "space", None),
    )
    return jax.shard_map(
        local,
        mesh=mesh,
        in_specs=placed,
        out_specs=P("member", None, "space", None),
        check_vma=False,
    )
```

```python
import functools
import math

import jax
import jax.numpy as jnp
from jax import lax
from jax.experimental import pallas as pl
from jax.experimental.pallas import tpu as pltpu
from jax.sharding import PartitionSpec as P

root_coef = math.sqrt(2.0 / math.pi)
cubic_coef = 0.044715
smooth = 0.25

CH = 32
RW = 8
W = 1024
FULL = CH * RW
EDGE = 4 * CH
PK = 64
PKT = 2 * PK + 8
bf16, f32 = jnp.bfloat16, jnp.float32


def iota(shape, dim):
    return lax.broadcasted_iota(jnp.int32, shape, dim)


def dot(a, b):
    return jnp.dot(a, b, preferred_element_type=f32)


def dot_nt(a, b):
    return lax.dot_general(a, b, (((1,), (1,)), ((), ())), preferred_element_type=f32)


def mod(a, n):
    return jnp.bitwise_and(a, n - 1)


def div(a, n):
    return lax.shift_right_logical(a, int(math.log2(n)))


def edge_row(e, odd):
    row = jnp.where(e < 2, e - 1, e + 5)
    return jnp.where(odd, 7 - row, row)


def facing(x):
    return jnp.bitwise_xor(x, 1)


def moved(x, step):
    zero = jnp.zeros((x.shape[0], 1), x.dtype)
    if step == 1:
        return jnp.concatenate([x[:, 1:], zero], axis=1)
    if step == -1:
        return jnp.concatenate([zero, x[:, :-1]], axis=1)
    return x


def gelu_pair(v):
    u = v * v
    h = 0.5 + 0.5 * jnp.tanh(v * (root_coef + (root_coef * cubic_coef) * u))
    slope = h + (v * (h - h * h)) * (2.0 * root_coef + (6.0 * root_coef * cubic_coef) * u)
    return v * h, slope


def smooth_slope(u):
    return u * lax.rsqrt(u * u + smooth * smooth)


def edge_rows(odd, weight):
    r, c = iota((EDGE, FULL), 0), iota((EDGE, FULL), 1)
    q = div(r, CH)
    top = (q < 2) != odd
    row = jnp.where(top, mod(q, 2), 7 - mod(q, 2))
    pick = ((div(c, RW) == mod(r, CH)) & (mod(c, RW) == row)).astype(f32).astype(bf16)
    r2, c2 = iota((2 * CH, FULL), 0), iota((2 * CH, FULL), 1)
    row = edge_row(1 + div(r2, CH), odd)
    pick2 = ((div(c2, RW) == mod(r2, CH)) & (mod(c2, RW) == row)).astype(f32).astype(bf16)
    blocks, none = [], jnp.zeros((CH, 2 * CH), f32)
    for d in range(3):
        low, mid, high = (weight[a * 3 + d].astype(f32) for a in range(3))
        one = jnp.concatenate([mid, jnp.where(odd, low, high), none], axis=1)
        two = jnp.concatenate([none, mid, jnp.where(odd, high, low)], axis=1)
        blocks.append(jnp.concatenate([one, two], axis=0))
    lend = jnp.concatenate(blocks, axis=1).astype(bf16)

    def rows(feat, skip):
        x = dot(pick, feat).astype(bf16)
        taps = jnp.concatenate([moved(x, d - 1) for d in range(3)], axis=0)
        return x, dot(lend, taps) + dot(pick2, skip)

    return rows


def pack_kernel(feat_in, skip_in, target_in, weight_in, one, two, lent, feat, skip, target, weight, sems):
    copies = [pltpu.make_async_copy(target_in, target, sems.at[4]), pltpu.make_async_copy(weight_in, weight, sems.at[5])]
    for m in range(2):
        copies.append(pltpu.make_async_copy(feat_in.at[m], feat.at[m], sems.at[m]))
        copies.append(pltpu.make_async_copy(skip_in.at[m], skip.at[m], sems.at[2 + m]))
    for copy in copies:
        copy.start()
    odd = mod(lax.axis_index("space"), 2) == 1
    copies[0].wait()
    copies[1].wait()
    line = iota((8, W), 0)
    for out, at, other in ((one, 0, 7), (two, 7, 0)):
        left = [jnp.where(odd, target[k + other : k + other + 1, :], target[k + at : k + at + 1, :]) for k in (0, 8)]
        total = jnp.zeros((8, W), f32)
        for term in range(3):
            for k in range(2):
                part = left[k].astype(bf16).astype(f32)
                left[k] = left[k] - part
                total = jnp.where(line == 2 * term + k, part, total)
        out[2 * PK : PKT] = total.astype(bf16)
    rows = edge_rows(odd, weight)
    for m in range(2):
        copies[2 + 2 * m].wait()
        copies[3 + 2 * m].wait()
        x, part = rows(feat[m], skip[m])
        lent[m] = part
        part = part.astype(bf16)
        one[m * PK : m * PK + 32] = x[0:32]
        two[m * PK : m * PK + 32] = x[64:96]
        one[m * PK + 32 : m * PK + 64] = part[:32]
        two[m * PK + 32 : m * PK + 64] = part[32:]


def mats_kernel(weight, out_weight, b_main, b_edge, b_back, p_main, p_edge, spread):
    place = lax.axis_index("space")
    odd = mod(place, 2) == 1
    ro = (div(iota((FULL, CH), 0), RW) == iota((FULL, CH), 1)).astype(f32).astype(bf16)
    re = (mod(iota((EDGE, CH), 0), CH) == iota((EDGE, CH), 1)).astype(f32).astype(bf16)
    r, c = iota((FULL, FULL), 0), iota((FULL, FULL), 1)
    row_of, row_at = mod(r, RW), mod(c, RW)
    inner = (row_at > 0) & (row_at < RW - 1)
    er, ec = div(iota((EDGE, EDGE), 0), CH), div(iota((EDGE, EDGE), 1), CH)
    step_edge = jnp.where(er == ec, edge_row(facing(er), odd) - edge_row(er, odd), 9)
    br, bc = iota((FULL, EDGE), 0), iota((FULL, EDGE), 1)
    step_back = mod(br, RW) - edge_row(div(bc, CH), odd)
    for d in range(3):
        main = jnp.zeros((FULL, FULL), f32)
        edge = jnp.zeros((EDGE, EDGE), f32)
        back = jnp.zeros((FULL, FULL), f32)
        back_edge = jnp.zeros((FULL, EDGE), f32)
        for a in range(3):
            w = weight[a * 3 + d]
            main = jnp.where(row_at - row_of == a - 1, dot_nt(dot(ro, w).astype(bf16), ro), main)
            edge = jnp.where(step_edge == a - 1, dot_nt(dot(re, w).astype(bf16), re), edge)
            t = dot_nt(ro, w).astype(bf16)
            back = jnp.where((row_of - row_at == a - 1) & inner, dot_nt(t, ro), back)
            back_edge = jnp.where(step_back == a - 1, dot_nt(t, re), back_edge)
        b_main[:, d * FULL : (d + 1) * FULL] = main.astype(bf16)
        b_edge[:, d * EDGE : (d + 1) * EDGE] = edge.astype(bf16)
        at = d * (FULL + EDGE)
        b_back[:, at : at + FULL] = back.astype(bf16)
        b_back[:, at + FULL : at + FULL + EDGE] = back_edge.astype(bf16)

    ow = out_weight[...].astype(f32)
    line = iota((32, CH), 0)
    second = jnp.where(line < 16, div(line, 8), mod(div(line, 2), 2)) == 1
    rows_w = jnp.where(second, ow[1:2, :], ow[0:1, :]).astype(bf16)
    pr, pc = iota((16, FULL), 0), iota((16, FULL), 1)
    same = (mod(pr, RW) == mod(pc, RW)) & (mod(pr, RW) > 0) & (mod(pr, RW) < RW - 1)
    p_main[...] = jnp.where(same, dot_nt(rows_w[:16], ro), 0.0).astype(bf16)

    def edge_match(line, e, m):
        inside = (line < 16) & (mod(line, 8) == edge_row(e, odd))
        outer = (div(line, 4) == 4 + m) & (e == jnp.where(mod(line, 2) == 0, 0, 3))
        return inside | outer

    lr, lc = iota((32, EDGE), 0), iota((32, EDGE), 1)
    wide = dot_nt(rows_w, re)
    for m in range(2):
        p_edge[m] = jnp.where(edge_match(lr, div(lc, CH), m), wide, 0.0).astype(bf16)
    sr, sc = iota((FULL, 32), 0), iota((FULL, 32), 1)
    whole = jnp.where((sc < 16) & (mod(sc, 8) == mod(sr, RW)), dot_nt(ro, rows_w), 0.0).astype(bf16)
    tr, tc = iota((EDGE, 32), 0), iota((EDGE, 32), 1)
    e = div(tr, CH)
    off = (e == 0) & ((place == 0) | (place == lax.axis_size("space") - 1))
    tall = dot_nt(re, rows_w)
    for m in range(2):
        spread[m, :FULL] = whole
        spread[m, FULL:] = jnp.where(edge_match(tc, e, m) & ~off, tall, 0.0).astype(bf16)


def main_kernel(feat, skip, b_main, p_main, slope, part, taps, pre, act):
    for m in range(2):
        x = feat[m]
        for d in range(3):
            taps[d * FULL : (d + 1) * FULL] = moved(x, d - 1)
        pre[...] = dot(b_main[...], taps[...])

        def rows(i, _):
            at = pl.ds(pl.multiple_of(i * 16, 16), 16)
            for half in range(2):
                cols = slice(half * 512, half * 512 + 512)
                a, s = gelu_pair(pre[at, cols] + skip[m, at, cols].astype(f32))
                act[at, cols] = a.astype(bf16)
                slope[m, at, cols] = s
            return 0

        lax.fori_loop(0, FULL // 16, rows, 0)
        part[m] = dot(p_main[...], act[...])


def edge_kernel(got_across, got_beside, across, beside, b_edge, p_edge, part, lent, slope, own, send, halo_target, taps, pre, act):
    halo = jnp.zeros((8, W), f32)
    for m in range(2):
        at = m * PK
        x = jnp.concatenate(
            [across[at : at + 32], got_across[at : at + 32], got_beside[at : at + 32], beside[at : at + 32]], axis=0
        )
        for d in range(3):
            taps[d * EDGE : (d + 1) * EDGE] = moved(x, d - 1)
        pre[...] = dot(b_edge[...], taps[...])
        for e in range(4):
            for step in range(2):
                rows = slice(e * CH + step * 16, e * CH + step * 16 + 16)
                far = slice(at + 32 + step * 16, at + 48 + step * 16)
                near = slice((e - 1) * CH + step * 16, (e - 1) * CH + step * 16 + 16)
                for half in range(2):
                    cols = slice(half * 512, half * 512 + 512)
                    if e in (1, 2):
                        base = lent[m, near, cols]
                    else:
                        base = (got_beside if e else got_across)[far, cols].astype(f32)
                    a, s = gelu_pair(pre[rows, cols] + base)
                    act[rows, cols] = a.astype(bf16)
                    slope[m, rows, cols] = s
        more = dot(p_edge[m], act[...])
        own[m * 16 : m * 16 + 16] = part[m] + more[:16]
        halo = halo + more[16:24]
    own[32:40] = halo
    both = jnp.concatenate([own[:, :512], own[:, 512:]], axis=0).astype(bf16)
    for k in range(8):
        send[k] = both
    line = iota((8, W), 0)
    total = jnp.zeros((8, W), f32)
    for h, source in enumerate((got_across, got_beside)):
        terms = source[2 * PK : PKT].astype(f32)
        for k in range(2):
            value = (terms[k : k + 1] + terms[2 + k : 3 + k]) + terms[4 + k : 5 + k]
            total = jnp.where(mod(line, 4) == 2 * k + h, value, total)
    halo_target[...] = total


def back_kernel(got, own, target, halo_target, slope, slope_edge, spread, b_back, out, grad, ga, taps, ready, sems):
    me = lax.axis_index("member")
    grad[...] = jnp.zeros(grad.shape, bf16)
    width = 256
    for c in range(512 // width):
        here = [slice(h * 512 + c * width, h * 512 + (c + 1) * width) for h in range(2)]
        mine, sums = [], []
        for h in range(2):
            o0, o1, oh = own[0:16, here[h]], own[16:32, here[h]], own[32:40, here[h]]
            t = smooth_slope(o0 - o1)
            mine.append((o0, o1, oh))
            sums.append([t, -t, smooth_slope(oh - jnp.concatenate([oh[4:], oh[:4]], axis=0))])
        for j in range(1, 8):
            theirs = got[mod(me + j, 8), :, c * width : (c + 1) * width].astype(f32)
            for h in range(2):
                o0, o1, oh = mine[h]
                x = theirs[40 * h : 40 * h + 40]
                x0, x1, xh = x[0:16], x[16:32], x[32:40]
                sums[h][0] += smooth_slope(o0 - x0) + smooth_slope(o0 - x1)
                sums[h][1] += smooth_slope(o1 - x0) + smooth_slope(o1 - x1)
                swapped = jnp.concatenate([xh[4:], xh[:4]], axis=0)
                sums[h][2] += smooth_slope(oh - xh) + smooth_slope(oh - swapped)
        for h in range(2):
            o0, o1, oh = mine[h]
            t = target[:, here[h]]
            gh = smooth_slope(oh - halo_target[:, here[h]]) - sums[h][2] * (1.0 / 15.0)
            tail = jnp.concatenate([gh, jnp.zeros_like(gh)], axis=0).astype(bf16)
            for m, o in enumerate((o0, o1)):
                grad[m, 0:16, here[h]] = (smooth_slope(o - t) - sums[h][m] * (1.0 / 15.0)).astype(bf16)
                grad[m, 16:32, here[h]] = tail
    size = FULL + EDGE
    copies = []
    for m in range(2):
        ga[m] = dot(spread[m], grad[m])
        for i in range(FULL // 16):
            at = slice(i * 16, i * 16 + 16)
            taps[m, size + i * 16 : size + i * 16 + 16] = (ga[m, at] * slope[m, at]).astype(bf16)
        for i in range(EDGE // 16):
            at = FULL + i * 16
            taps[m, size + at : size + at + 16] = (ga[m, at : at + 16] * slope_edge[m, i * 16 : i * 16 + 16]).astype(bf16)
        g = taps[m, size : 2 * size]
        taps[m, 0:size] = moved(g, 1)
        taps[m, 2 * size : 3 * size] = moved(g, -1)
    for m in range(2):
        for h in range(2):
            cols = slice(h * 512, h * 512 + 512)
            ready[m, :, cols] = dot(b_back[...], taps[m, :, cols]).astype(bf16)
            copy = pltpu.make_async_copy(ready.at[m, :, cols], out.at[m, :, cols], sems.at[2 * m + h])
            copy.start()
            copies.append(copy)
    for copy in copies:
        copy.wait()


def call(kernel, outs, scratch, flops, *args, far=(), far_out=False, grant=32):
    near = pl.BlockSpec(memory_space=pltpu.VMEM)
    hbm = pl.BlockSpec(memory_space=pltpu.HBM)
    args = [pltpu.with_memory_space_constraint(x, pltpu.HBM) if i in far else x for i, x in enumerate(args)]
    return pl.pallas_call(
        kernel,
        out_shape=outs,
        in_specs=[hbm if i in far else near for i in range(len(args))],
        out_specs=[hbm if far_out else near] * len(outs),
        scratch_shapes=scratch,
        compiler_params=pltpu.CompilerParams(vmem_limit_bytes=grant * 1024 * 1024),
        cost_estimate=pl.CostEstimate(flops=flops, bytes_accessed=1 << 20, transcendentals=0),
    )(*args)


def local(features, skip, conv_weight, out_weight, target):
    S = jax.ShapeDtypeStruct
    V = pltpu.VMEM
    feat = features.reshape(2, FULL, W)
    bypass = skip.reshape(2, FULL, W)
    goal = target.reshape(16, W)
    weight = conv_weight.reshape(9, CH, CH)
    dma = pltpu.SemaphoreType.DMA
    across, beside, lent = call(
        pack_kernel,
        [S((PKT, W), bf16), S((PKT, W), bf16), S((2, 2 * CH, W), f32)],
        [
            V((2, FULL, W), bf16),
            V((2, FULL, W), bf16),
            V((16, W), f32),
            V((9, CH, CH), bf16),
            dma((6,)),
        ],
        1 << 29,
        feat,
        bypass,
        goal,
        weight,
        far=(0, 1, 2, 3),
    )
    count = lax.axis_size("space")
    got_across = lax.ppermute(across, "space", [(i, ((i + 1) ^ 1) - 1) for i in range(1, count - 1)])
    got_beside = lax.ppermute(beside, "space", [(i, i ^ 1) for i in range(count)])
    b_main, b_edge, b_back, p_main, p_edge, spread = call(
        mats_kernel,
        [
            S((FULL, 3 * FULL), bf16),
            S((EDGE, 3 * EDGE), bf16),
            S((FULL, 3 * (FULL + EDGE)), bf16),
            S((16, FULL), bf16),
            S((2, 32, EDGE), bf16),
            S((2, FULL + EDGE, 32), bf16),
        ],
        [],
        1 << 31,
        weight,
        out_weight,
    )
    slope, part = call(
        main_kernel,
        [S((2, FULL, W), f32), S((2, 16, W), f32)],
        [V((3 * FULL, W), bf16), V((FULL, W), f32), V((FULL, W), bf16)],
        1 << 31,
        feat,
        bypass,
        b_main,
        p_main,
    )
    slope_edge, own, send, halo_target = call(
        edge_kernel,
        [S((2, EDGE, W), f32), S((40, W), f32), S((8, 80, 512), bf16), S((8, W), f32)],
        [V((3 * EDGE, W), bf16), V((EDGE, W), f32), V((EDGE, W), bf16)],
        1 << 30,
        got_across,
        got_beside,
        across,
        beside,
        b_edge,
        p_edge,
        part,
        lent,
    )
    got = lax.all_to_all(send, "member", split_axis=0, concat_axis=0, tiled=True)
    size = FULL + EDGE
    (out,) = call(
        back_kernel,
        [S((2, FULL, W), bf16)],
        [
            V((2, 32, W), bf16),
            V((2, size, W), f32),
            V((2, 3 * size, W), bf16),
            V((2, FULL, W), bf16),
            dma((4,)),
        ],
        1 << 31,
        got,
        own,
        goal,
        halo_target,
        slope,
        slope_edge,
        spread,
        b_back,
        far_out=True,
    )
    return out.reshape(2, CH, RW, W)


def solution(mesh):
    placed = (
        P("member", None, "space", None),
        P("member", None, "space", None),
        P(),
        P(),
        P(None, "space", None),
    )
    return jax.shard_map(
        local,
        mesh=mesh,
        in_specs=placed,
        out_specs=P("member", None, "space", None),
        check_vma=False,
    )
```

```python
import functools
import math

import jax
import jax.numpy as jnp
from jax import lax
from jax.experimental import pallas as pl
from jax.experimental.pallas import tpu as pltpu
from jax.sharding import PartitionSpec as P

root_coef = math.sqrt(2.0 / math.pi)
cubic_coef = 0.044715
smooth = 0.25

CH = 32
RW = 8
W = 1024
FULL = CH * RW
EDGE = 4 * CH
PK = 64
PKT = 2 * PK + 8
bf16, f32 = jnp.bfloat16, jnp.float32


def iota(shape, dim):
    return lax.broadcasted_iota(jnp.int32, shape, dim)


def dot(a, b):
    return jnp.dot(a, b, preferred_element_type=f32)


def dot_nt(a, b):
    return lax.dot_general(a, b, (((1,), (1,)), ((), ())), preferred_element_type=f32)


def mod(a, n):
    return jnp.bitwise_and(a, n - 1)


def div(a, n):
    return lax.shift_right_logical(a, int(math.log2(n)))


def edge_row(e, odd):
    row = jnp.where(e < 2, e - 1, e + 5)
    return jnp.where(odd, 7 - row, row)


def facing(x):
    return jnp.bitwise_xor(x, 1)


def moved(x, step):
    zero = jnp.zeros((x.shape[0], 1), x.dtype)
    if step == 1:
        return jnp.concatenate([x[:, 1:], zero], axis=1)
    if step == -1:
        return jnp.concatenate([zero, x[:, :-1]], axis=1)
    return x


def gelu_pair(v):
    u = v * v
    h = 0.5 + 0.5 * jnp.tanh(v * (root_coef + (root_coef * cubic_coef) * u))
    slope = h + (v * (h - h * h)) * (2.0 * root_coef + (6.0 * root_coef * cubic_coef) * u)
    return v * h, slope


def smooth_slope(u):
    return u * lax.rsqrt(u * u + smooth * smooth)


def edge_rows(odd, weight):
    r, c = iota((EDGE, FULL), 0), iota((EDGE, FULL), 1)
    q = div(r, CH)
    top = (q < 2) != odd
    row = jnp.where(top, mod(q, 2), 7 - mod(q, 2))
    pick = ((div(c, RW) == mod(r, CH)) & (mod(c, RW) == row)).astype(f32).astype(bf16)
    r2, c2 = iota((2 * CH, FULL), 0), iota((2 * CH, FULL), 1)
    row = edge_row(1 + div(r2, CH), odd)
    pick2 = ((div(c2, RW) == mod(r2, CH)) & (mod(c2, RW) == row)).astype(f32).astype(bf16)
    blocks, none = [], jnp.zeros((CH, 2 * CH), f32)
    for d in range(3):
        low, mid, high = (weight[a * 3 + d].astype(f32) for a in range(3))
        one = jnp.concatenate([mid, jnp.where(odd, low, high), none], axis=1)
        two = jnp.concatenate([none, mid, jnp.where(odd, high, low)], axis=1)
        blocks += [one, two]
    lend = dot(jnp.concatenate(blocks, axis=0).astype(bf16), pick)
    pick = pick.astype(f32)
    every = jnp.concatenate([lend, pick[0:32], pick[64:96]], axis=0).astype(bf16)

    def rows(feat, skip):
        y = dot(every, feat)
        part = (moved(y[0:64], -1) + y[64:128]) + (moved(y[128:192], 1) + dot(pick2, skip))
        return y[192:256].astype(bf16), part

    return rows


def pack_kernel(feat_in, skip_in, target_in, weight_in, one, two, lent, feat, skip, target, weight, sems):
    copies = [pltpu.make_async_copy(target_in, target, sems.at[4]), pltpu.make_async_copy(weight_in, weight, sems.at[5])]
    for m in range(2):
        copies.append(pltpu.make_async_copy(feat_in.at[m], feat.at[m], sems.at[m]))
        copies.append(pltpu.make_async_copy(skip_in.at[m], skip.at[m], sems.at[2 + m]))
    for copy in copies:
        copy.start()
    odd = mod(lax.axis_index("space"), 2) == 1
    copies[0].wait()
    copies[1].wait()
    line = iota((8, W), 0)
    for out, at, other in ((one, 0, 7), (two, 7, 0)):
        left = [jnp.where(odd, target[k + other : k + other + 1, :], target[k + at : k + at + 1, :]) for k in (0, 8)]
        total = jnp.zeros((8, W), f32)
        for term in range(3):
            for k in range(2):
                part = left[k].astype(bf16).astype(f32)
                left[k] = left[k] - part
                total = jnp.where(line == 2 * term + k, part, total)
        out[2 * PK : PKT] = total.astype(bf16)
    rows = edge_rows(odd, weight)
    for m in range(2):
        copies[2 + 2 * m].wait()
        copies[3 + 2 * m].wait()
        x, part = rows(feat[m], skip[m])
        lent[m] = part
        part = part.astype(bf16)
        one[m * PK : m * PK + 32] = x[0:32]
        two[m * PK : m * PK + 32] = x[32:64]
        one[m * PK + 32 : m * PK + 64] = part[:32]
        two[m * PK + 32 : m * PK + 64] = part[32:]


def mats_kernel(weight, out_weight, b_main, b_edge, b_back, p_main, p_edge, spread, rows):
    place = lax.axis_index("space")
    odd = mod(place, 2) == 1
    ro = (div(iota((FULL, CH), 0), RW) == iota((FULL, CH), 1)).astype(f32).astype(bf16)
    re = (mod(iota((EDGE, CH), 0), CH) == iota((EDGE, CH), 1)).astype(f32).astype(bf16)
    r, c = iota((FULL, FULL), 0), iota((FULL, FULL), 1)
    swap = ((div(r, RW) == mod(c, CH)) & (mod(r, RW) == div(c, CH))).astype(f32).astype(bf16)
    same = (r == c).astype(f32).astype(bf16)
    inner = (mod(r, RW) > 0) & (mod(r, RW) < RW - 1)
    half = 2 * CH
    er, ec = div(iota((half, half), 0), CH), div(iota((half, half), 1), CH)
    steps = [jnp.where(er == ec, edge_row(facing(e), odd) - edge_row(e, odd), 9) for e in (3 * er, 1 + er)]
    br, bc = iota((FULL, EDGE), 0), iota((FULL, EDGE), 1)
    step_back = mod(br, RW) - edge_row(div(bc, CH), odd)
    for d in range(3):
        taps = [weight[a * 3 + d].astype(f32) for a in range(3)]
        for row in range(RW):
            blocks = [taps[at - row + 1] if abs(at - row) <= 1 else jnp.zeros((CH, CH), f32) for at in range(RW)]
            whole = jnp.concatenate([jnp.concatenate(blocks[i : i + 4], axis=1) for i in (0, 4)], axis=1)
            rows[row * CH : (row + 1) * CH, d * FULL : (d + 1) * FULL] = whole.astype(bf16)
    turned = dot(swap, rows[...]).astype(bf16)
    for d in range(3):
        main = dot_nt(turned[:, d * FULL : (d + 1) * FULL], swap)
        b_main[:, d * FULL : (d + 1) * FULL] = main.astype(bf16)
        at = d * (FULL + EDGE)
        b_back[:, at : at + FULL] = dot_nt(same, jnp.where(inner, main, 0.0).astype(bf16)).astype(bf16)
        edges = [jnp.zeros((half, half), f32)] * 2
        back_edge = jnp.zeros((FULL, EDGE), f32)
        for a in range(3):
            w = weight[a * 3 + d]
            spot = dot_nt(dot(re[:half], w).astype(bf16), re[:half])
            edges = [jnp.where(step == a - 1, spot, edge) for step, edge in zip(steps, edges)]
            back_edge = jnp.where(step_back == a - 1, dot_nt(dot_nt(ro, w).astype(bf16), re), back_edge)
        for i in range(2):
            b_edge[i, d] = edges[i].astype(bf16)
        b_back[:, at + FULL : at + FULL + EDGE] = back_edge.astype(bf16)

    ow = out_weight[...].astype(f32)
    line = iota((32, CH), 0)
    second = jnp.where(line < 16, div(line, 8), mod(div(line, 2), 2)) == 1
    rows_w = jnp.where(second, ow[1:2, :], ow[0:1, :]).astype(bf16)
    pr, pc = iota((16, FULL), 0), iota((16, FULL), 1)
    kept = (mod(pr, RW) == mod(pc, RW)) & (mod(pr, RW) > 0) & (mod(pr, RW) < RW - 1)
    p_main[...] = jnp.where(kept, dot_nt(rows_w[:16], ro), 0.0).astype(bf16)

    def edge_match(line, e, m):
        inside = (line < 16) & (mod(line, 8) == edge_row(e, odd))
        outer = (div(line, 4) == 4 + m) & (e == jnp.where(mod(line, 2) == 0, 0, 3))
        return inside | outer

    lr, lc = iota((32, EDGE), 0), iota((32, EDGE), 1)
    wide = dot_nt(rows_w, re)
    for m in range(2):
        p_edge[m] = jnp.where(edge_match(lr, div(lc, CH), m), wide, 0.0).astype(bf16)
    sr, sc = iota((FULL, 32), 0), iota((FULL, 32), 1)
    whole = jnp.where((sc < 16) & (mod(sc, 8) == mod(sr, RW)), dot_nt(ro, rows_w), 0.0).astype(bf16)
    tr, tc = iota((EDGE, 32), 0), iota((EDGE, 32), 1)
    e = div(tr, CH)
    off = (e == 0) & ((place == 0) | (place == lax.axis_size("space") - 1))
    tall = dot_nt(re, rows_w)
    for m in range(2):
        spread[m, :FULL] = whole
        spread[m, FULL:] = jnp.where(edge_match(tc, e, m) & ~off, tall, 0.0).astype(bf16)


def main_kernel(feat, skip, across, beside, b_main, b_edge, p_main, slope, part, outer, taps, pre, act):
    for m in range(2):
        x = feat[m]
        for d in range(3):
            taps[d * FULL : (d + 1) * FULL] = moved(x, d - 1)
        pre[...] = dot(b_main[...], taps[...])

        def rows(i, _):
            at = pl.ds(pl.multiple_of(i * 16, 16), 16)
            for half in range(2):
                cols = slice(half * 512, half * 512 + 512)
                a, s = gelu_pair(pre[at, cols] + skip[m, at, cols].astype(f32))
                act[at, cols] = a.astype(bf16)
                slope[m, at, cols] = s
            return 0

        lax.fori_loop(0, FULL // 16, rows, 0)
        part[m] = dot(p_main[...], act[...])
        at = m * PK
        x = jnp.concatenate([across[at : at + 32], beside[at : at + 32]], axis=0)
        outer[m] = sum(dot(b_edge[0, d], moved(x, d - 1)) for d in range(3))


def edge_kernel(got_across, got_beside, b_edge, p_edge, part, lent, outer, slope, own, send, halo_target, pre, act):
    halo = jnp.zeros((8, W), f32)
    for m in range(2):
        at = m * PK
        x = jnp.concatenate([got_across[at : at + 32], got_beside[at : at + 32]], axis=0)
        pre[...] = sum(dot(b_edge[1, d], moved(x, d - 1)) for d in range(3)) + lent[m]
        for e in range(4):
            for step in range(2):
                rows = slice(e * CH + step * 16, e * CH + step * 16 + 16)
                far = slice(at + 32 + step * 16, at + 48 + step * 16)
                inner = slice((e - 1) * CH + step * 16, (e - 1) * CH + step * 16 + 16)
                ends = slice(e // 3 * CH + step * 16, e // 3 * CH + step * 16 + 16)
                for half in range(2):
                    cols = slice(half * 512, half * 512 + 512)
                    if e in (1, 2):
                        v = pre[inner, cols]
                    else:
                        v = outer[m, ends, cols] + (got_beside if e else got_across)[far, cols].astype(f32)
                    a, s = gelu_pair(v)
                    act[rows, cols] = a.astype(bf16)
                    slope[m, rows, cols] = s
        more = dot(p_edge[m], act[...])
        own[m * 16 : m * 16 + 16] = part[m] + more[:16]
        halo = halo + more[16:24]
    own[32:40] = halo
    both = jnp.concatenate([own[:, :512], own[:, 512:]], axis=0).astype(bf16)
    for k in range(8):
        send[k] = both
    line = iota((8, W), 0)
    total = jnp.zeros((8, W), f32)
    for h, source in enumerate((got_across, got_beside)):
        terms = source[2 * PK : PKT].astype(f32)
        for k in range(2):
            value = (terms[k : k + 1] + terms[2 + k : 3 + k]) + terms[4 + k : 5 + k]
            total = jnp.where(mod(line, 4) == 2 * k + h, value, total)
    halo_target[...] = total


def back_kernel(got, own, target, halo_target, slope, slope_edge, spread, b_back, out, grad, ga, taps, ready, sems):
    me = lax.axis_index("member")
    grad[...] = jnp.zeros(grad.shape, bf16)
    width = 256
    for c in range(512 // width):
        here = [slice(h * 512 + c * width, h * 512 + (c + 1) * width) for h in range(2)]
        mine, sums = [], []
        for h in range(2):
            o0, o1, oh = own[0:16, here[h]], own[16:32, here[h]], own[32:40, here[h]]
            t = smooth_slope(o0 - o1)
            mine.append((o0, o1, oh))
            sums.append([t, -t, smooth_slope(oh - jnp.concatenate([oh[4:], oh[:4]], axis=0))])
        for j in range(1, 8):
            theirs = got[mod(me + j, 8), :, c * width : (c + 1) * width].astype(f32)
            for h in range(2):
                o0, o1, oh = mine[h]
                x = theirs[40 * h : 40 * h + 40]
                x0, x1, xh = x[0:16], x[16:32], x[32:40]
                sums[h][0] += smooth_slope(o0 - x0) + smooth_slope(o0 - x1)
                sums[h][1] += smooth_slope(o1 - x0) + smooth_slope(o1 - x1)
                swapped = jnp.concatenate([xh[4:], xh[:4]], axis=0)
                sums[h][2] += smooth_slope(oh - xh) + smooth_slope(oh - swapped)
        for h in range(2):
            o0, o1, oh = mine[h]
            t = target[:, here[h]]
            gh = smooth_slope(oh - halo_target[:, here[h]]) - sums[h][2] * (1.0 / 15.0)
            tail = jnp.concatenate([gh, jnp.zeros_like(gh)], axis=0).astype(bf16)
            for m, o in enumerate((o0, o1)):
                grad[m, 0:16, here[h]] = (smooth_slope(o - t) - sums[h][m] * (1.0 / 15.0)).astype(bf16)
                grad[m, 16:32, here[h]] = tail
    size = FULL + EDGE
    copies = []
    for m in range(2):
        ga[m] = dot(spread[m], grad[m])
        for i in range(FULL // 16):
            at = slice(i * 16, i * 16 + 16)
            taps[m, size + i * 16 : size + i * 16 + 16] = (ga[m, at] * slope[m, at]).astype(bf16)
        for i in range(EDGE // 16):
            at = FULL + i * 16
            taps[m, size + at : size + at + 16] = (ga[m, at : at + 16] * slope_edge[m, i * 16 : i * 16 + 16]).astype(bf16)
        g = taps[m, size : 2 * size]
        taps[m, 0:size] = moved(g, 1)
        taps[m, 2 * size : 3 * size] = moved(g, -1)
    for m in range(2):
        for h in range(2):
            cols = slice(h * 512, h * 512 + 512)
            ready[m, :, cols] = dot(b_back[...], taps[m, :, cols]).astype(bf16)
            copy = pltpu.make_async_copy(ready.at[m, :, cols], out.at[m, :, cols], sems.at[2 * m + h])
            copy.start()
            copies.append(copy)
    for copy in copies:
        copy.wait()


def call(kernel, outs, scratch, flops, *args, far=(), far_out=False, grant=32):
    near = pl.BlockSpec(memory_space=pltpu.VMEM)
    hbm = pl.BlockSpec(memory_space=pltpu.HBM)
    args = [pltpu.with_memory_space_constraint(x, pltpu.HBM) if i in far else x for i, x in enumerate(args)]
    return pl.pallas_call(
        kernel,
        out_shape=outs,
        in_specs=[hbm if i in far else near for i in range(len(args))],
        out_specs=[hbm if far_out else near] * len(outs),
        scratch_shapes=scratch,
        compiler_params=pltpu.CompilerParams(vmem_limit_bytes=grant * 1024 * 1024),
        cost_estimate=pl.CostEstimate(flops=flops, bytes_accessed=1 << 20, transcendentals=0),
    )(*args)


def local(features, skip, conv_weight, out_weight, target):
    S = jax.ShapeDtypeStruct
    V = pltpu.VMEM
    feat = features.reshape(2, FULL, W)
    bypass = skip.reshape(2, FULL, W)
    goal = target.reshape(16, W)
    weight = conv_weight.reshape(9, CH, CH)
    dma = pltpu.SemaphoreType.DMA
    across, beside, lent = call(
        pack_kernel,
        [S((PKT, W), bf16), S((PKT, W), bf16), S((2, 2 * CH, W), f32)],
        [
            V((2, FULL, W), bf16),
            V((2, FULL, W), bf16),
            V((16, W), f32),
            V((9, CH, CH), bf16),
            dma((6,)),
        ],
        1 << 29,
        feat,
        bypass,
        goal,
        weight,
        far=(0, 1, 2, 3),
    )
    count = lax.axis_size("space")
    got_across = lax.ppermute(across, "space", [(i, ((i + 1) ^ 1) - 1) for i in range(1, count - 1)])
    got_beside = lax.ppermute(beside, "space", [(i, i ^ 1) for i in range(count)])
    b_main, b_edge, b_back, p_main, p_edge, spread = call(
        mats_kernel,
        [
            S((FULL, 3 * FULL), bf16),
            S((2, 3, 2 * CH, 2 * CH), bf16),
            S((FULL, 3 * (FULL + EDGE)), bf16),
            S((16, FULL), bf16),
            S((2, 32, EDGE), bf16),
            S((2, FULL + EDGE, 32), bf16),
        ],
        [V((FULL, 3 * FULL), bf16)],
        1 << 31,
        weight,
        out_weight,
    )
    slope, part, outer = call(
        main_kernel,
        [S((2, FULL, W), f32), S((2, 16, W), f32), S((2, 2 * CH, W), f32)],
        [V((3 * FULL, W), bf16), V((FULL, W), f32), V((FULL, W), bf16)],
        1 << 31,
        feat,
        bypass,
        across,
        beside,
        b_main,
        b_edge,
        p_main,
    )
    slope_edge, own, send, halo_target = call(
        edge_kernel,
        [S((2, EDGE, W), f32), S((40, W), f32), S((8, 80, 512), bf16), S((8, W), f32)],
        [V((2 * CH, W), f32), V((EDGE, W), bf16)],
        1 << 30,
        got_across,
        got_beside,
        b_edge,
        p_edge,
        part,
        lent,
        outer,
    )
    got = lax.all_to_all(send, "member", split_axis=0, concat_axis=0, tiled=True)
    size = FULL + EDGE
    (out,) = call(
        back_kernel,
        [S((2, FULL, W), bf16)],
        [
            V((2, 32, W), bf16),
            V((2, size, W), f32),
            V((2, 3 * size, W), bf16),
            V((2, FULL, W), bf16),
            dma((4,)),
        ],
        1 << 31,
        got,
        own,
        goal,
        halo_target,
        slope,
        slope_edge,
        spread,
        b_back,
        far_out=True,
    )
    return out.reshape(2, CH, RW, W)


def solution(mesh):
    placed = (
        P("member", None, "space", None),
        P("member", None, "space", None),
        P(),
        P(),
        P(None, "space", None),
    )
    return jax.shard_map(
        local,
        mesh=mesh,
        in_specs=placed,
        out_specs=P("member", None, "space", None),
        check_vma=False,
    )
```

```python
import functools
import math

import jax
import jax.numpy as jnp
from jax import lax
from jax.experimental import pallas as pl
from jax.experimental.pallas import tpu as pltpu
from jax.sharding import PartitionSpec as P

root_coef = math.sqrt(2.0 / math.pi)
cubic_coef = 0.044715
smooth = 0.25

CH = 32
RW = 8
W = 1024
FULL = CH * RW
EDGE = 4 * CH
PK = 64
PKT = 2 * PK + 8
bf16, f32 = jnp.bfloat16, jnp.float32


def iota(shape, dim):
    return lax.broadcasted_iota(jnp.int32, shape, dim)


def dot(a, b):
    return jnp.dot(a, b, preferred_element_type=f32)


def dot_nt(a, b):
    return lax.dot_general(a, b, (((1,), (1,)), ((), ())), preferred_element_type=f32)


def mod(a, n):
    return jnp.bitwise_and(a, n - 1)


def div(a, n):
    return lax.shift_right_logical(a, int(math.log2(n)))


def edge_row(e, odd):
    row = jnp.where(e < 2, e - 1, e + 5)
    return jnp.where(odd, 7 - row, row)


def facing(x):
    return jnp.bitwise_xor(x, 1)


def moved(x, step):
    zero = jnp.zeros((x.shape[0], 1), x.dtype)
    if step == 1:
        return jnp.concatenate([x[:, 1:], zero], axis=1)
    if step == -1:
        return jnp.concatenate([zero, x[:, :-1]], axis=1)
    return x


def three(matrix, x):
    y, n = dot(matrix, x), CH
    return moved(y[0:n], -1) + y[n : 2 * n] + moved(y[2 * n : 3 * n], 1)


def gelu_pair(v):
    u = v * v
    h = 0.5 + 0.5 * jnp.tanh(v * (root_coef + (root_coef * cubic_coef) * u))
    slope = h + (v * (h - h * h)) * (2.0 * root_coef + (6.0 * root_coef * cubic_coef) * u)
    return v * h, slope


def smooth_slope(u):
    return u * lax.rsqrt(u * u + smooth * smooth)


def edge_rows(odd, weight):
    r, c = iota((EDGE, FULL), 0), iota((EDGE, FULL), 1)
    q = div(r, CH)
    top = (q < 2) != odd
    row = jnp.where(top, mod(q, 2), 7 - mod(q, 2))
    pick = ((div(c, RW) == mod(r, CH)) & (mod(c, RW) == row)).astype(f32).astype(bf16)
    r2, c2 = iota((2 * CH, FULL), 0), iota((2 * CH, FULL), 1)
    row = edge_row(1 + div(r2, CH), odd)
    pick2 = ((div(c2, RW) == mod(r2, CH)) & (mod(c2, RW) == row)).astype(f32).astype(bf16)
    blocks, none = [], jnp.zeros((CH, 2 * CH), f32)
    for d in range(3):
        low, mid, high = (weight[a * 3 + d].astype(f32) for a in range(3))
        one = jnp.concatenate([mid, jnp.where(odd, low, high), none], axis=1)
        two = jnp.concatenate([none, mid, jnp.where(odd, high, low)], axis=1)
        blocks += [one, two]
    lend = dot(jnp.concatenate(blocks, axis=0).astype(bf16), pick)
    pick = pick.astype(f32)
    every = jnp.concatenate([lend, pick[0:32], pick[64:96]], axis=0).astype(bf16)

    def rows(feat, skip):
        y = dot(every, feat)
        part = (moved(y[0:64], -1) + y[64:128]) + (moved(y[128:192], 1) + dot(pick2, skip))
        return y[192:256].astype(bf16), part

    return rows


def pack_kernel(feat_in, skip_in, target_in, weight_in, one, two, lent, feat, skip, target, weight, sems):
    copies = [pltpu.make_async_copy(target_in, target, sems.at[4]), pltpu.make_async_copy(weight_in, weight, sems.at[5])]
    for m in range(2):
        copies.append(pltpu.make_async_copy(feat_in.at[m], feat.at[m], sems.at[m]))
        copies.append(pltpu.make_async_copy(skip_in.at[m], skip.at[m], sems.at[2 + m]))
    for copy in copies:
        copy.start()
    odd = mod(lax.axis_index("space"), 2) == 1
    copies[0].wait()
    copies[1].wait()
    line = iota((8, W), 0)
    for out, at, other in ((one, 0, 7), (two, 7, 0)):
        left = [jnp.where(odd, target[k + other : k + other + 1, :], target[k + at : k + at + 1, :]) for k in (0, 8)]
        total = jnp.zeros((8, W), f32)
        for term in range(3):
            for k in range(2):
                part = left[k].astype(bf16).astype(f32)
                left[k] = left[k] - part
                total = jnp.where(line == 2 * term + k, part, total)
        out[2 * PK : PKT] = total.astype(bf16)
    rows = edge_rows(odd, weight)
    for m in range(2):
        copies[2 + 2 * m].wait()
        copies[3 + 2 * m].wait()
        x, part = rows(feat[m], skip[m])
        lent[m] = part
        part = part.astype(bf16)
        one[m * PK : m * PK + 32] = x[0:32]
        two[m * PK : m * PK + 32] = x[32:64]
        one[m * PK + 32 : m * PK + 64] = part[:32]
        two[m * PK + 32 : m * PK + 64] = part[32:]


def mats_kernel(weight, out_weight, b_main, b_edge, b_back, p_main, p_edge, spread, rows):
    place = lax.axis_index("space")
    odd = mod(place, 2) == 1
    ro = (div(iota((FULL, CH), 0), RW) == iota((FULL, CH), 1)).astype(f32).astype(bf16)
    re = (mod(iota((EDGE, CH), 0), CH) == iota((EDGE, CH), 1)).astype(f32).astype(bf16)
    r, c = iota((FULL, FULL), 0), iota((FULL, FULL), 1)
    swap = ((div(r, RW) == mod(c, CH)) & (mod(r, RW) == div(c, CH))).astype(f32).astype(bf16)
    same = (r == c).astype(f32).astype(bf16)
    inner = (mod(r, RW) > 0) & (mod(r, RW) < RW - 1)
    br, bc = iota((FULL, EDGE), 0), iota((FULL, EDGE), 1)
    step_back = mod(br, RW) - edge_row(div(bc, CH), odd)
    taps_of = [[weight[a * 3 + d].astype(f32) for a in range(3)] for d in range(3)]
    for d in range(3):
        taps = taps_of[d]
        for row in range(RW):
            blocks = [taps[at - row + 1] if abs(at - row) <= 1 else jnp.zeros((CH, CH), f32) for at in range(RW)]
            whole = jnp.concatenate([jnp.concatenate(blocks[i : i + 4], axis=1) for i in (0, 4)], axis=1)
            rows[row * CH : (row + 1) * CH, d * FULL : (d + 1) * FULL] = whole.astype(bf16)
    turned = dot(swap, rows[...]).astype(bf16)
    for d in range(3):
        main = dot_nt(turned[:, d * FULL : (d + 1) * FULL], swap)
        b_main[:, d * FULL : (d + 1) * FULL] = main.astype(bf16)
        at = d * (FULL + EDGE)
        b_back[:, at : at + FULL] = dot_nt(same, jnp.where(inner, main, 0.0).astype(bf16)).astype(bf16)
        back_edge = jnp.zeros((FULL, EDGE), f32)
        for a in range(3):
            w = weight[a * 3 + d]
            back_edge = jnp.where(step_back == a - 1, dot_nt(dot_nt(ro, w).astype(bf16), re), back_edge)
        high = jnp.where(odd, taps_of[d][0], taps_of[d][2]).astype(bf16)
        low = jnp.where(odd, taps_of[d][2], taps_of[d][0]).astype(bf16)
        for i, j, w in ((0, 0, high), (1, 0, low), (1, 1, high), (0, 1, low)):
            b_edge[i, j, d * CH : (d + 1) * CH] = w
        b_back[:, at + FULL : at + FULL + EDGE] = back_edge.astype(bf16)

    ow = out_weight[...].astype(f32)
    line = iota((32, CH), 0)
    second = jnp.where(line < 16, div(line, 8), mod(div(line, 2), 2)) == 1
    rows_w = jnp.where(second, ow[1:2, :], ow[0:1, :]).astype(bf16)
    pr, pc = iota((16, FULL), 0), iota((16, FULL), 1)
    kept = (mod(pr, RW) == mod(pc, RW)) & (mod(pr, RW) > 0) & (mod(pr, RW) < RW - 1)
    p_main[...] = jnp.where(kept, dot_nt(rows_w[:16], ro), 0.0).astype(bf16)

    def edge_match(line, e, m):
        inside = (line < 16) & (mod(line, 8) == edge_row(e, odd))
        outer = (div(line, 4) == 4 + m) & (e == jnp.where(mod(line, 2) == 0, 0, 3))
        return inside | outer

    lr, lc = iota((32, EDGE), 0), iota((32, EDGE), 1)
    wide = dot_nt(rows_w, re)
    for m in range(2):
        both = jnp.where(edge_match(lr, div(lc, CH), m), wide, 0.0)
        for i in range(2):
            p_edge[m, i] = both[:, i * 64 : i * 64 + 64].astype(bf16)
    sr, sc = iota((FULL, 32), 0), iota((FULL, 32), 1)
    whole = jnp.where((sc < 16) & (mod(sc, 8) == mod(sr, RW)), dot_nt(ro, rows_w), 0.0).astype(bf16)
    tr, tc = iota((EDGE, 32), 0), iota((EDGE, 32), 1)
    e = div(tr, CH)
    off = (e == 0) & ((place == 0) | (place == lax.axis_size("space") - 1))
    tall = dot_nt(re, rows_w)
    for m in range(2):
        spread[m, :FULL] = whole
        spread[m, FULL:] = jnp.where(edge_match(tc, e, m) & ~off, tall, 0.0).astype(bf16)


def main_kernel(feat, skip, across, beside, b_main, b_edge, p_main, slope, part, outer, taps, pre, act):
    for m in range(2):
        x = feat[m]
        for d in range(3):
            taps[d * FULL : (d + 1) * FULL] = moved(x, d - 1)
        pre[...] = dot(b_main[...], taps[...])

        def rows(i, _):
            at = pl.ds(pl.multiple_of(i * 16, 16), 16)
            for half in range(2):
                cols = slice(half * 512, half * 512 + 512)
                a, s = gelu_pair(pre[at, cols] + skip[m, at, cols].astype(f32))
                act[at, cols] = a.astype(bf16)
                slope[m, at, cols] = s
            return 0

        lax.fori_loop(0, FULL // 16, rows, 0)
        part[m] = dot(p_main[...], act[...])
        at = m * PK
        outer[m, 0:32] = three(b_edge[0, 0], across[at : at + 32])
        outer[m, 32:64] = three(b_edge[0, 1], beside[at : at + 32])


def side(i, m, got, b_edge, p_edge, lent, outer, slope, pre, act):
    at = m * PK
    pre[0:32] = outer[m, i * 32 : i * 32 + 32] + got[at + 32 : at + 64].astype(f32)
    pre[32:64] = three(b_edge[1, i], got[at : at + 32]) + lent[m, i * 32 : i * 32 + 32]
    for step in range(4):
        near = slice(step * 16, step * 16 + 16)
        to = (step + 2 * i) % 4 * 16
        rows = slice(to, to + 16)
        for half in range(2):
            cols = slice(half * 512, half * 512 + 512)
            a, s = gelu_pair(pre[near, cols])
            act[rows, cols] = a.astype(bf16)
            slope[m, rows, cols] = s
    return dot(p_edge[m, i], act[...])


def halo_goal(h, got, rest):
    line = iota((8, W), 0)
    terms = got[2 * PK : PKT].astype(f32)
    for k in range(2):
        value = (terms[k : k + 1] + terms[2 + k : 3 + k]) + terms[4 + k : 5 + k]
        rest = jnp.where(mod(line, 4) == 2 * k + h, value, rest)
    return rest


def beside_kernel(got, b_edge, p_edge, part, lent, outer, slope, own, halo_target, pre, act):
    halo = jnp.zeros((8, W), f32)
    for m in range(2):
        more = side(1, m, got, b_edge, p_edge, lent, outer, slope, pre, act)
        own[m * 16 : m * 16 + 16] = part[m] + more[:16]
        halo = halo + more[16:24]
    own[32:40] = halo
    halo_target[...] = halo_goal(1, got, jnp.zeros((8, W), f32))


def across_kernel(got, b_edge, p_edge, lent, outer, some, some_target, slope, own, send, halo_target, pre, act):
    halo = some[32:40]
    for m in range(2):
        more = side(0, m, got, b_edge, p_edge, lent, outer, slope, pre, act)
        own[m * 16 : m * 16 + 16] = some[m * 16 : m * 16 + 16] + more[:16]
        halo = halo + more[16:24]
    own[32:40] = halo
    both = jnp.concatenate([own[:, :512], own[:, 512:]], axis=0).astype(bf16)
    for k in range(8):
        send[k] = both
    halo_target[...] = halo_goal(0, got, some_target[...])


def back_kernel(got, own, target, halo_target, slope, slope_across, slope_beside, spread, b_back, out, grad, ga, taps, ready, sems):
    me = lax.axis_index("member")
    grad[...] = jnp.zeros(grad.shape, bf16)
    width = 256
    for c in range(512 // width):
        here = [slice(h * 512 + c * width, h * 512 + (c + 1) * width) for h in range(2)]
        mine, sums = [], []
        for h in range(2):
            o0, o1, oh = own[0:16, here[h]], own[16:32, here[h]], own[32:40, here[h]]
            t = smooth_slope(o0 - o1)
            mine.append((o0, o1, oh))
            sums.append([t, -t, smooth_slope(oh - jnp.concatenate([oh[4:], oh[:4]], axis=0))])
        for j in range(1, 8):
            theirs = got[mod(me + j, 8), :, c * width : (c + 1) * width].astype(f32)
            for h in range(2):
                o0, o1, oh = mine[h]
                x = theirs[40 * h : 40 * h + 40]
                x0, x1, xh = x[0:16], x[16:32], x[32:40]
                sums[h][0] += smooth_slope(o0 - x0) + smooth_slope(o0 - x1)
                sums[h][1] += smooth_slope(o1 - x0) + smooth_slope(o1 - x1)
                swapped = jnp.concatenate([xh[4:], xh[:4]], axis=0)
                sums[h][2] += smooth_slope(oh - xh) + smooth_slope(oh - swapped)
        for h in range(2):
            o0, o1, oh = mine[h]
            t = target[:, here[h]]
            gh = smooth_slope(oh - halo_target[:, here[h]]) - sums[h][2] * (1.0 / 15.0)
            tail = jnp.concatenate([gh, jnp.zeros_like(gh)], axis=0).astype(bf16)
            for m, o in enumerate((o0, o1)):
                grad[m, 0:16, here[h]] = (smooth_slope(o - t) - sums[h][m] * (1.0 / 15.0)).astype(bf16)
                grad[m, 16:32, here[h]] = tail
    size = FULL + EDGE
    copies = []
    for m in range(2):
        ga[m] = dot(spread[m], grad[m])
        for i in range(FULL // 16):
            at = slice(i * 16, i * 16 + 16)
            taps[m, size + i * 16 : size + i * 16 + 16] = (ga[m, at] * slope[m, at]).astype(bf16)
        for i in range(EDGE // 16):
            at = FULL + i * 16
            edge = (slope_beside if i > 3 else slope_across)[m, i % 4 * 16 : i % 4 * 16 + 16]
            taps[m, size + at : size + at + 16] = (ga[m, at : at + 16] * edge).astype(bf16)
        g = taps[m, size : 2 * size]
        taps[m, 0:size] = moved(g, 1)
        taps[m, 2 * size : 3 * size] = moved(g, -1)
    for m in range(2):
        for h in range(2):
            cols = slice(h * 512, h * 512 + 512)
            ready[m, :, cols] = dot(b_back[...], taps[m, :, cols]).astype(bf16)
            copy = pltpu.make_async_copy(ready.at[m, :, cols], out.at[m, :, cols], sems.at[2 * m + h])
            copy.start()
            copies.append(copy)
    for copy in copies:
        copy.wait()


def call(kernel, outs, scratch, flops, *args, far=(), far_out=False, grant=32):
    near = pl.BlockSpec(memory_space=pltpu.VMEM)
    hbm = pl.BlockSpec(memory_space=pltpu.HBM)
    args = [pltpu.with_memory_space_constraint(x, pltpu.HBM) if i in far else x for i, x in enumerate(args)]
    return pl.pallas_call(
        kernel,
        out_shape=outs,
        in_specs=[hbm if i in far else near for i in range(len(args))],
        out_specs=[hbm if far_out else near] * len(outs),
        scratch_shapes=scratch,
        compiler_params=pltpu.CompilerParams(vmem_limit_bytes=grant * 1024 * 1024),
        cost_estimate=pl.CostEstimate(flops=flops, bytes_accessed=1 << 20, transcendentals=0),
    )(*args)


def local(features, skip, conv_weight, out_weight, target):
    S = jax.ShapeDtypeStruct
    V = pltpu.VMEM
    feat = features.reshape(2, FULL, W)
    bypass = skip.reshape(2, FULL, W)
    goal = target.reshape(16, W)
    weight = conv_weight.reshape(9, CH, CH)
    dma = pltpu.SemaphoreType.DMA
    across, beside, lent = call(
        pack_kernel,
        [S((PKT, W), bf16), S((PKT, W), bf16), S((2, 2 * CH, W), f32)],
        [
            V((2, FULL, W), bf16),
            V((2, FULL, W), bf16),
            V((16, W), f32),
            V((9, CH, CH), bf16),
            dma((6,)),
        ],
        1 << 29,
        feat,
        bypass,
        goal,
        weight,
        far=(0, 1, 2, 3),
    )
    count = lax.axis_size("space")
    got_across = lax.ppermute(across, "space", [(i, ((i + 1) ^ 1) - 1) for i in range(1, count - 1)])
    got_beside = lax.ppermute(beside, "space", [(i, i ^ 1) for i in range(count)])
    b_main, b_edge, b_back, p_main, p_edge, spread = call(
        mats_kernel,
        [
            S((FULL, 3 * FULL), bf16),
            S((2, 2, 3 * CH, CH), bf16),
            S((FULL, 3 * (FULL + EDGE)), bf16),
            S((16, FULL), bf16),
            S((2, 2, 32, 2 * CH), bf16),
            S((2, FULL + EDGE, 32), bf16),
        ],
        [V((FULL, 3 * FULL), bf16)],
        1 << 31,
        weight,
        out_weight,
    )
    slope, part, outer = call(
        main_kernel,
        [S((2, FULL, W), f32), S((2, 16, W), f32), S((2, 2 * CH, W), f32)],
        [V((3 * FULL, W), bf16), V((FULL, W), f32), V((FULL, W), bf16)],
        1 << 31,
        feat,
        bypass,
        across,
        beside,
        b_main,
        b_edge,
        p_main,
    )
    slope_beside, some, some_target = call(
        beside_kernel,
        [S((2, 2 * CH, W), f32), S((40, W), f32), S((8, W), f32)],
        [V((2 * CH, W), f32), V((2 * CH, W), bf16)],
        1 << 29,
        got_beside,
        b_edge,
        p_edge,
        part,
        lent,
        outer,
    )
    slope_across, own, send, halo_target = call(
        across_kernel,
        [S((2, 2 * CH, W), f32), S((40, W), f32), S((8, 80, 512), bf16), S((8, W), f32)],
        [V((2 * CH, W), f32), V((2 * CH, W), bf16)],
        1 << 29,
        got_across,
        b_edge,
        p_edge,
        lent,
        outer,
        some,
        some_target,
    )
    got = lax.all_to_all(send, "member", split_axis=0, concat_axis=0, tiled=True)
    size = FULL + EDGE
    (out,) = call(
        back_kernel,
        [S((2, FULL, W), bf16)],
        [
            V((2, 32, W), bf16),
            V((2, size, W), f32),
            V((2, 3 * size, W), bf16),
            V((2, FULL, W), bf16),
            dma((4,)),
        ],
        1 << 31,
        got,
        own,
        goal,
        halo_target,
        slope,
        slope_across,
        slope_beside,
        spread,
        b_back,
        far_out=True,
    )
    return out.reshape(2, CH, RW, W)


def solution(mesh):
    placed = (
        P("member", None, "space", None),
        P("member", None, "space", None),
        P(),
        P(),
        P(None, "space", None),
    )
    return jax.shard_map(
        local,
        mesh=mesh,
        in_specs=placed,
        out_specs=P("member", None, "space", None),
        check_vma=False,
    )
```

```python
import functools
import math

import jax
import jax.numpy as jnp
from jax import lax
from jax.experimental import pallas as pl
from jax.experimental.pallas import tpu as pltpu
from jax.sharding import PartitionSpec as P

root_coef = math.sqrt(2.0 / math.pi)
cubic_coef = 0.044715
smooth = 0.25

CH = 32
RW = 8
W = 1024
FULL = CH * RW
EDGE = 4 * CH
PK = 64
PKT = 2 * PK + 8
bf16, f32 = jnp.bfloat16, jnp.float32


def iota(shape, dim):
    return lax.broadcasted_iota(jnp.int32, shape, dim)


def dot(a, b):
    return jnp.dot(a, b, preferred_element_type=f32)


def dot_nt(a, b):
    return lax.dot_general(a, b, (((1,), (1,)), ((), ())), preferred_element_type=f32)


def mod(a, n):
    return jnp.bitwise_and(a, n - 1)


def div(a, n):
    return lax.shift_right_logical(a, int(math.log2(n)))


def edge_row(e, odd):
    row = jnp.where(e < 2, e - 1, e + 5)
    return jnp.where(odd, 7 - row, row)


def facing(x):
    return jnp.bitwise_xor(x, 1)


def moved(x, step):
    zero = jnp.zeros((x.shape[0], 1), x.dtype)
    if step == 1:
        return jnp.concatenate([x[:, 1:], zero], axis=1)
    if step == -1:
        return jnp.concatenate([zero, x[:, :-1]], axis=1)
    return x


def three(matrix, x):
    y, n = dot(matrix, x), CH
    return moved(y[0:n], -1) + y[n : 2 * n] + moved(y[2 * n : 3 * n], 1)


def gelu_pair(v):
    u = v * v
    h = 0.5 + 0.5 * jnp.tanh(v * (root_coef + (root_coef * cubic_coef) * u))
    slope = h + (v * (h - h * h)) * (2.0 * root_coef + (6.0 * root_coef * cubic_coef) * u)
    return v * h, slope


def smooth_slope(u):
    return u * lax.rsqrt(u * u + smooth * smooth)


def edge_rows(odd, weight):
    r, c = iota((EDGE, FULL), 0), iota((EDGE, FULL), 1)
    q = div(r, CH)
    top = (q < 2) != odd
    row = jnp.where(top, mod(q, 2), 7 - mod(q, 2))
    pick = ((div(c, RW) == mod(r, CH)) & (mod(c, RW) == row)).astype(f32).astype(bf16)
    r2, c2 = iota((2 * CH, FULL), 0), iota((2 * CH, FULL), 1)
    row = edge_row(1 + div(r2, CH), odd)
    pick2 = ((div(c2, RW) == mod(r2, CH)) & (mod(c2, RW) == row)).astype(f32).astype(bf16)
    blocks, none = [], jnp.zeros((CH, 2 * CH), f32)
    for d in range(3):
        low, mid, high = (weight[a * 3 + d].astype(f32) for a in range(3))
        one = jnp.concatenate([mid, jnp.where(odd, low, high), none], axis=1)
        two = jnp.concatenate([none, mid, jnp.where(odd, high, low)], axis=1)
        blocks += [one, two]
    lend = dot(jnp.concatenate(blocks, axis=0).astype(bf16), pick)
    pick = pick.astype(f32)
    every = jnp.concatenate([lend, pick[0:32], pick[64:96]], axis=0).astype(bf16)

    def rows(feat, skip):
        y = dot(every, feat)
        part = (moved(y[0:64], -1) + y[64:128]) + (moved(y[128:192], 1) + dot(pick2, skip))
        return y[192:256].astype(bf16), part

    return rows


def pack_kernel(feat_in, skip_in, target_in, weight_in, one, two, lent, feat, skip, target, weight, sems):
    copies = [pltpu.make_async_copy(target_in, target, sems.at[4]), pltpu.make_async_copy(weight_in, weight, sems.at[5])]
    for m in range(2):
        copies.append(pltpu.make_async_copy(feat_in.at[m], feat.at[m], sems.at[m]))
        copies.append(pltpu.make_async_copy(skip_in.at[m], skip.at[m], sems.at[2 + m]))
    for copy in copies:
        copy.start()
    odd = mod(lax.axis_index("space"), 2) == 1
    copies[0].wait()
    copies[1].wait()
    line = iota((8, W), 0)
    for out, at, other in ((one, 0, 7), (two, 7, 0)):
        left = [jnp.where(odd, target[k + other : k + other + 1, :], target[k + at : k + at + 1, :]) for k in (0, 8)]
        total = jnp.zeros((8, W), f32)
        for term in range(3):
            for k in range(2):
                part = left[k].astype(bf16).astype(f32)
                left[k] = left[k] - part
                total = jnp.where(line == 2 * term + k, part, total)
        out[2 * PK : PKT] = total.astype(bf16)
    rows = edge_rows(odd, weight)
    for m in range(2):
        copies[2 + 2 * m].wait()
        copies[3 + 2 * m].wait()
        x, part = rows(feat[m], skip[m])
        lent[m] = part
        part = part.astype(bf16)
        one[m * PK : m * PK + 32] = x[0:32]
        two[m * PK : m * PK + 32] = x[32:64]
        one[m * PK + 32 : m * PK + 64] = part[:32]
        two[m * PK + 32 : m * PK + 64] = part[32:]


def mats_kernel(weight, out_weight, b_main, b_edge, b_back, p_main, p_edge, spread, columns, rows):
    place = lax.axis_index("space")
    odd = mod(place, 2) == 1
    ro = (div(iota((FULL, CH), 0), RW) == iota((FULL, CH), 1)).astype(f32).astype(bf16)
    re = (mod(iota((EDGE, CH), 0), CH) == iota((EDGE, CH), 1)).astype(f32).astype(bf16)
    r, c = iota((FULL, FULL), 0), iota((FULL, FULL), 1)
    swap = ((div(r, RW) == mod(c, CH)) & (mod(r, RW) == div(c, CH))).astype(f32).astype(bf16)
    same = (r == c).astype(f32).astype(bf16)
    inner = (mod(r, RW) > 0) & (mod(r, RW) < RW - 1)
    br, bc = iota((FULL, EDGE), 0), iota((FULL, EDGE), 1)
    step_back = mod(br, RW) - edge_row(div(bc, CH), odd)
    taps_of = [[weight[a * 3 + d].astype(f32) for a in range(3)] for d in range(3)]
    for d in range(3):
        taps = taps_of[d]
        for row in range(RW):
            blocks = [taps[at - row + 1] if abs(at - row) <= 1 else jnp.zeros((CH, CH), f32) for at in range(RW)]
            whole = jnp.concatenate([jnp.concatenate(blocks[i : i + 4], axis=1) for i in (0, 4)], axis=1)
            rows[row * CH : (row + 1) * CH, d * FULL : (d + 1) * FULL] = whole.astype(bf16)
    turned = dot(swap, rows[...]).astype(bf16)
    for d in range(3):
        main = dot_nt(turned[:, d * FULL : (d + 1) * FULL], swap)
        b_main[:, d * FULL : (d + 1) * FULL] = main.astype(bf16)
        at = d * (FULL + EDGE)
        b_back[:, at : at + FULL] = dot_nt(same, jnp.where(inner, main, 0.0).astype(bf16)).astype(bf16)
        back_edge = jnp.zeros((FULL, EDGE), f32)
        for a in range(3):
            w = weight[a * 3 + d]
            back_edge = jnp.where(step_back == a - 1, dot_nt(dot_nt(ro, w).astype(bf16), re), back_edge)
        high = jnp.where(odd, taps_of[d][0], taps_of[d][2]).astype(bf16)
        low = jnp.where(odd, taps_of[d][2], taps_of[d][0]).astype(bf16)
        for i, j, w in ((0, 0, high), (1, 0, low), (1, 1, high), (0, 1, low)):
            b_edge[i, j, d * CH : (d + 1) * CH] = w
        b_back[:, at + FULL : at + FULL + EDGE] = back_edge.astype(bf16)

    ow = out_weight[...].astype(f32)
    line = iota((32, CH), 0)
    second = jnp.where(line < 16, div(line, 8), mod(div(line, 2), 2)) == 1
    rows_w = jnp.where(second, ow[1:2, :], ow[0:1, :]).astype(bf16)
    pr, pc = iota((16, FULL), 0), iota((16, FULL), 1)
    kept = (mod(pr, RW) == mod(pc, RW)) & (mod(pr, RW) > 0) & (mod(pr, RW) < RW - 1)
    p_main[...] = jnp.where(kept, dot_nt(rows_w[:16], ro), 0.0).astype(bf16)

    def edge_match(line, e, m):
        inside = (line < 16) & (mod(line, 8) == edge_row(e, odd))
        outer = (div(line, 4) == 4 + m) & (e == jnp.where(mod(line, 2) == 0, 0, 3))
        return inside | outer

    lr, lc = iota((32, EDGE), 0), iota((32, EDGE), 1)
    wide = dot_nt(rows_w, re)
    for m in range(2):
        both = jnp.where(edge_match(lr, div(lc, CH), m), wide, 0.0)
        for i in range(2):
            p_edge[m, i] = both[:, i * 64 : i * 64 + 64].astype(bf16)
    for k in range(2):
        columns[k] = dot_nt(ro, jnp.broadcast_to(ow[k : k + 1, :], (128, CH)).astype(bf16))
    tr, tc = iota((EDGE, 32), 0), iota((EDGE, 32), 1)
    e = div(tr, CH)
    off = (e == 0) & ((place == 0) | (place == lax.axis_size("space") - 1))
    tall = dot_nt(re, rows_w)
    for m in range(2):
        spread[m] = jnp.where(edge_match(tc, e, m) & ~off, tall, 0.0).astype(bf16)


def main_kernel(feat, skip, across, beside, b_main, b_edge, p_main, slope, part, outer, taps, pre, act):
    for m in range(2):
        x = feat[m]
        for d in range(3):
            taps[d * FULL : (d + 1) * FULL] = moved(x, d - 1)
        pre[...] = dot(b_main[...], taps[...])

        def rows(i, _):
            at = pl.ds(pl.multiple_of(i * 16, 16), 16)
            for half in range(2):
                cols = slice(half * 512, half * 512 + 512)
                a, s = gelu_pair(pre[at, cols] + skip[m, at, cols].astype(f32))
                act[at, cols] = a.astype(bf16)
                slope[m, at, cols] = s
            return 0

        lax.fori_loop(0, FULL // 16, rows, 0)
        part[m] = dot(p_main[...], act[...])
        at = m * PK
        outer[m, 0:32] = three(b_edge[0, 0], across[at : at + 32])
        outer[m, 32:64] = three(b_edge[0, 1], beside[at : at + 32])


def side(i, m, got, b_edge, p_edge, lent, outer, slope, pre, act):
    at = m * PK
    pre[0:32] = outer[m, i * 32 : i * 32 + 32] + got[at + 32 : at + 64].astype(f32)
    pre[32:64] = three(b_edge[1, i], got[at : at + 32]) + lent[m, i * 32 : i * 32 + 32]
    for step in range(4):
        near = slice(step * 16, step * 16 + 16)
        to = (step + 2 * i) % 4 * 16
        rows = slice(to, to + 16)
        for half in range(2):
            cols = slice(half * 512, half * 512 + 512)
            a, s = gelu_pair(pre[near, cols])
            act[rows, cols] = a.astype(bf16)
            slope[m, rows, cols] = s
    return dot(p_edge[m, i], act[...])


def halo_goal(h, got, rest):
    line = iota((8, W), 0)
    terms = got[2 * PK : PKT].astype(f32)
    for k in range(2):
        value = (terms[k : k + 1] + terms[2 + k : 3 + k]) + terms[4 + k : 5 + k]
        rest = jnp.where(mod(line, 4) == 2 * k + h, value, rest)
    return rest


def beside_kernel(got, b_edge, p_edge, part, lent, outer, slope, own, halo_target, pre, act):
    halo = jnp.zeros((8, W), f32)
    for m in range(2):
        more = side(1, m, got, b_edge, p_edge, lent, outer, slope, pre, act)
        own[m * 16 : m * 16 + 16] = part[m] + more[:16]
        halo = halo + more[16:24]
    own[32:40] = halo
    halo_target[...] = halo_goal(1, got, jnp.zeros((8, W), f32))


def across_kernel(got, b_edge, p_edge, lent, outer, some, some_target, slope, own, send, halo_target, pre, act):
    halo = some[32:40]
    for m in range(2):
        more = side(0, m, got, b_edge, p_edge, lent, outer, slope, pre, act)
        own[m * 16 : m * 16 + 16] = some[m * 16 : m * 16 + 16] + more[:16]
        halo = halo + more[16:24]
    own[32:40] = halo
    both = jnp.concatenate([own[:, :512], own[:, 512:]], axis=0).astype(bf16)
    for k in range(8):
        send[k] = both
    halo_target[...] = halo_goal(0, got, some_target[...])


def back_kernel(got, own, target, halo_target, slope, slope_across, slope_beside, spread, columns, b_back, out, grad, plain, ga, taps, ready, sems):
    me = lax.axis_index("member")
    grad[...] = jnp.zeros(grad.shape, bf16)
    width = 256
    for c in range(512 // width):
        here = [slice(h * 512 + c * width, h * 512 + (c + 1) * width) for h in range(2)]
        mine, sums = [], []
        for h in range(2):
            o0, o1, oh = own[0:16, here[h]], own[16:32, here[h]], own[32:40, here[h]]
            t = smooth_slope(o0 - o1)
            mine.append((o0, o1, oh))
            sums.append([t, -t, smooth_slope(oh - jnp.concatenate([oh[4:], oh[:4]], axis=0))])
        for j in range(1, 8):
            theirs = got[mod(me + j, 8), :, c * width : (c + 1) * width].astype(f32)
            for h in range(2):
                o0, o1, oh = mine[h]
                x = theirs[40 * h : 40 * h + 40]
                x0, x1, xh = x[0:16], x[16:32], x[32:40]
                sums[h][0] += smooth_slope(o0 - x0) + smooth_slope(o0 - x1)
                sums[h][1] += smooth_slope(o1 - x0) + smooth_slope(o1 - x1)
                swapped = jnp.concatenate([xh[4:], xh[:4]], axis=0)
                sums[h][2] += smooth_slope(oh - xh) + smooth_slope(oh - swapped)
        for h in range(2):
            o0, o1, oh = mine[h]
            t = target[:, here[h]]
            gh = smooth_slope(oh - halo_target[:, here[h]]) - sums[h][2] * (1.0 / 15.0)
            tail = jnp.concatenate([gh, jnp.zeros_like(gh)], axis=0).astype(bf16)
            for m, o in enumerate((o0, o1)):
                g = (smooth_slope(o - t) - sums[h][m] * (1.0 / 15.0)).astype(bf16)
                grad[m, 0:16, here[h]] = g
                plain[m, :, here[h]] = g.astype(f32)
                grad[m, 16:32, here[h]] = tail
    size = FULL + EDGE
    copies = []
    for m in range(2):
        ga[m] = dot(spread[m], grad[m])
        for h in range(2):
            cols = slice(h * 512, h * 512 + 512)
            g0, g1 = (jnp.concatenate([plain[m, k : k + 8, cols]] * 2, axis=0) for k in (0, 8))
            for i in range(FULL // 16):
                at = slice(i * 16, i * 16 + 16)
                w0, w1 = (jnp.concatenate([columns[k, at]] * 4, axis=1) for k in range(2))
                taps[m, size + i * 16 : size + i * 16 + 16, cols] = ((w0 * g0 + w1 * g1) * slope[m, at, cols]).astype(bf16)
        for i in range(EDGE // 16):
            at = FULL + i * 16
            edge = (slope_beside if i > 3 else slope_across)[m, i % 4 * 16 : i % 4 * 16 + 16]
            taps[m, size + at : size + at + 16] = (ga[m, i * 16 : i * 16 + 16] * edge).astype(bf16)
        g = taps[m, size : 2 * size]
        taps[m, 0:size] = moved(g, 1)
        taps[m, 2 * size : 3 * size] = moved(g, -1)
    for m in range(2):
        for h in range(2):
            cols = slice(h * 512, h * 512 + 512)
            ready[m, :, cols] = dot(b_back[...], taps[m, :, cols]).astype(bf16)
            copy = pltpu.make_async_copy(ready.at[m, :, cols], out.at[m, :, cols], sems.at[2 * m + h])
            copy.start()
            copies.append(copy)
    for copy in copies:
        copy.wait()


def call(kernel, outs, scratch, flops, *args, far=(), far_out=False, grant=32):
    near = pl.BlockSpec(memory_space=pltpu.VMEM)
    hbm = pl.BlockSpec(memory_space=pltpu.HBM)
    args = [pltpu.with_memory_space_constraint(x, pltpu.HBM) if i in far else x for i, x in enumerate(args)]
    return pl.pallas_call(
        kernel,
        out_shape=outs,
        in_specs=[hbm if i in far else near for i in range(len(args))],
        out_specs=[hbm if far_out else near] * len(outs),
        scratch_shapes=scratch,
        compiler_params=pltpu.CompilerParams(vmem_limit_bytes=grant * 1024 * 1024),
        cost_estimate=pl.CostEstimate(flops=flops, bytes_accessed=1 << 20, transcendentals=0),
    )(*args)


def local(features, skip, conv_weight, out_weight, target):
    S = jax.ShapeDtypeStruct
    V = pltpu.VMEM
    feat = features.reshape(2, FULL, W)
    bypass = skip.reshape(2, FULL, W)
    goal = target.reshape(16, W)
    weight = conv_weight.reshape(9, CH, CH)
    dma = pltpu.SemaphoreType.DMA
    across, beside, lent = call(
        pack_kernel,
        [S((PKT, W), bf16), S((PKT, W), bf16), S((2, 2 * CH, W), f32)],
        [
            V((2, FULL, W), bf16),
            V((2, FULL, W), bf16),
            V((16, W), f32),
            V((9, CH, CH), bf16),
            dma((6,)),
        ],
        1 << 29,
        feat,
        bypass,
        goal,
        weight,
        far=(0, 1, 2, 3),
    )
    count = lax.axis_size("space")
    got_across = lax.ppermute(across, "space", [(i, ((i + 1) ^ 1) - 1) for i in range(1, count - 1)])
    got_beside = lax.ppermute(beside, "space", [(i, i ^ 1) for i in range(count)])
    b_main, b_edge, b_back, p_main, p_edge, spread, columns = call(
        mats_kernel,
        [
            S((FULL, 3 * FULL), bf16),
            S((2, 2, 3 * CH, CH), bf16),
            S((FULL, 3 * (FULL + EDGE)), bf16),
            S((16, FULL), bf16),
            S((2, 2, 32, 2 * CH), bf16),
            S((2, EDGE, 32), bf16),
            S((2, FULL, 128), f32),
        ],
        [V((FULL, 3 * FULL), bf16)],
        1 << 31,
        weight,
        out_weight,
    )
    slope, part, outer = call(
        main_kernel,
        [S((2, FULL, W), f32), S((2, 16, W), f32), S((2, 2 * CH, W), f32)],
        [V((3 * FULL, W), bf16), V((FULL, W), f32), V((FULL, W), bf16)],
        1 << 31,
        feat,
        bypass,
        across,
        beside,
        b_main,
        b_edge,
        p_main,
    )
    slope_beside, some, some_target = call(
        beside_kernel,
        [S((2, 2 * CH, W), f32), S((40, W), f32), S((8, W), f32)],
        [V((2 * CH, W), f32), V((2 * CH, W), bf16)],
        1 << 29,
        got_beside,
        b_edge,
        p_edge,
        part,
        lent,
        outer,
    )
    slope_across, own, send, halo_target = call(
        across_kernel,
        [S((2, 2 * CH, W), f32), S((40, W), f32), S((8, 80, 512), bf16), S((8, W), f32)],
        [V((2 * CH, W), f32), V((2 * CH, W), bf16)],
        1 << 29,
        got_across,
        b_edge,
        p_edge,
        lent,
        outer,
        some,
        some_target,
    )
    got = lax.all_to_all(send, "member", split_axis=0, concat_axis=0, tiled=True)
    size = FULL + EDGE
    (out,) = call(
        back_kernel,
        [S((2, FULL, W), bf16)],
        [
            V((2, 32, W), bf16),
            V((2, 16, W), f32),
            V((2, EDGE, W), f32),
            V((2, 3 * size, W), bf16),
            V((2, FULL, W), bf16),
            dma((4,)),
        ],
        1 << 31,
        got,
        own,
        goal,
        halo_target,
        slope,
        slope_across,
        slope_beside,
        spread,
        columns,
        b_back,
        far_out=True,
    )
    return out.reshape(2, CH, RW, W)


def solution(mesh):
    placed = (
        P("member", None, "space", None),
        P("member", None, "space", None),
        P(),
        P(),
        P(None, "space", None),
    )
    return jax.shard_map(
        local,
        mesh=mesh,
        in_specs=placed,
        out_specs=P("member", None, "space", None),
        check_vma=False,
    )
```

```python
import functools
import math

import jax
import jax.numpy as jnp
from jax import lax
from jax.experimental import pallas as pl
from jax.experimental.pallas import tpu as pltpu
from jax.sharding import PartitionSpec as P

root_coef = math.sqrt(2.0 / math.pi)
cubic_coef = 0.044715
smooth = 0.25

CH = 32
RW = 8
W = 1024
FULL = CH * RW
EDGE = 4 * CH
PK = 64
PKT = 2 * PK + 8
bf16, f32 = jnp.bfloat16, jnp.float32


def iota(shape, dim):
    return lax.broadcasted_iota(jnp.int32, shape, dim)


def dot(a, b):
    return jnp.dot(a, b, preferred_element_type=f32)


def dot_nt(a, b):
    return lax.dot_general(a, b, (((1,), (1,)), ((), ())), preferred_element_type=f32)


def mod(a, n):
    return jnp.bitwise_and(a, n - 1)


def div(a, n):
    return lax.shift_right_logical(a, int(math.log2(n)))


def edge_row(e, odd):
    row = jnp.where(e < 2, e - 1, e + 5)
    return jnp.where(odd, 7 - row, row)


def facing(x):
    return jnp.bitwise_xor(x, 1)


def moved(x, step):
    zero = jnp.zeros((x.shape[0], 1), x.dtype)
    if step == 1:
        return jnp.concatenate([x[:, 1:], zero], axis=1)
    if step == -1:
        return jnp.concatenate([zero, x[:, :-1]], axis=1)
    return x


def three(matrix, x):
    y, n = dot(matrix, x), CH
    return moved(y[0:n], -1) + y[n : 2 * n] + moved(y[2 * n : 3 * n], 1)


def gelu_pair(v):
    u = v * v
    h = 0.5 + 0.5 * jnp.tanh(v * (root_coef + (root_coef * cubic_coef) * u))
    slope = h + (v * (h - h * h)) * (2.0 * root_coef + (6.0 * root_coef * cubic_coef) * u)
    return v * h, slope


def smooth_slope(u):
    return u * lax.rsqrt(u * u + smooth * smooth)


def edge_rows(odd, weight):
    r, c = iota((EDGE, FULL), 0), iota((EDGE, FULL), 1)
    q = div(r, CH)
    top = (q < 2) != odd
    row = jnp.where(top, mod(q, 2), 7 - mod(q, 2))
    pick = ((div(c, RW) == mod(r, CH)) & (mod(c, RW) == row)).astype(f32).astype(bf16)
    r2, c2 = iota((2 * CH, FULL), 0), iota((2 * CH, FULL), 1)
    row = edge_row(1 + div(r2, CH), odd)
    pick2 = ((div(c2, RW) == mod(r2, CH)) & (mod(c2, RW) == row)).astype(f32).astype(bf16)
    blocks, none = [], jnp.zeros((CH, 2 * CH), f32)
    for d in range(3):
        low, mid, high = (weight[a * 3 + d].astype(f32) for a in range(3))
        one = jnp.concatenate([mid, jnp.where(odd, low, high), none], axis=1)
        two = jnp.concatenate([none, mid, jnp.where(odd, high, low)], axis=1)
        blocks += [one, two]
    lend = dot(jnp.concatenate(blocks, axis=0).astype(bf16), pick)
    pick = pick.astype(f32)
    every = jnp.concatenate([lend, pick[0:32], pick[64:96]], axis=0).astype(bf16)

    def rows(feat, skip):
        y = dot(every, feat)
        part = (moved(y[0:64], -1) + y[64:128]) + (moved(y[128:192], 1) + dot(pick2, skip))
        return y[192:256].astype(bf16), part

    return rows


def pack_kernel(feat_in, skip_in, target_in, weight_in, one, two, lent, feat, skip, target, weight, sems):
    copies = [pltpu.make_async_copy(target_in, target, sems.at[4]), pltpu.make_async_copy(weight_in, weight, sems.at[5])]
    for m in range(2):
        copies.append(pltpu.make_async_copy(feat_in.at[m], feat.at[m], sems.at[m]))
        copies.append(pltpu.make_async_copy(skip_in.at[m], skip.at[m], sems.at[2 + m]))
    for copy in copies:
        copy.start()
    odd = mod(lax.axis_index("space"), 2) == 1
    copies[0].wait()
    copies[1].wait()
    line = iota((8, W), 0)
    for out, at, other in ((one, 0, 7), (two, 7, 0)):
        left = [jnp.where(odd, target[k + other : k + other + 1, :], target[k + at : k + at + 1, :]) for k in (0, 8)]
        total = jnp.zeros((8, W), f32)
        for term in range(3):
            for k in range(2):
                part = left[k].astype(bf16).astype(f32)
                left[k] = left[k] - part
                total = jnp.where(line == 2 * term + k, part, total)
        out[2 * PK : PKT] = total.astype(bf16)
    rows = edge_rows(odd, weight)
    for m in range(2):
        copies[2 + 2 * m].wait()
        copies[3 + 2 * m].wait()
        x, part = rows(feat[m], skip[m])
        lent[m] = part
        part = part.astype(bf16)
        one[m * PK : m * PK + 32] = x[0:32]
        two[m * PK : m * PK + 32] = x[32:64]
        one[m * PK + 32 : m * PK + 64] = part[:32]
        two[m * PK + 32 : m * PK + 64] = part[32:]


def mats_kernel(weight, out_weight, b_main, b_edge, b_back, p_main, p_edge, spread, columns, rows):
    place = lax.axis_index("space")
    odd = mod(place, 2) == 1
    ro = (div(iota((FULL, CH), 0), RW) == iota((FULL, CH), 1)).astype(f32).astype(bf16)
    re = (mod(iota((EDGE, CH), 0), CH) == iota((EDGE, CH), 1)).astype(f32).astype(bf16)
    r, c = iota((FULL, FULL), 0), iota((FULL, FULL), 1)
    swap = ((div(r, RW) == mod(c, CH)) & (mod(r, RW) == div(c, CH))).astype(f32).astype(bf16)
    same = (r == c).astype(f32).astype(bf16)
    inner = (mod(r, RW) > 0) & (mod(r, RW) < RW - 1)
    br, bc = iota((FULL, EDGE), 0), iota((FULL, EDGE), 1)
    step_back = mod(br, RW) - edge_row(div(bc, CH), odd)
    taps_of = [[weight[a * 3 + d].astype(f32) for a in range(3)] for d in range(3)]
    for d in range(3):
        taps = taps_of[d]
        for row in range(RW):
            blocks = [taps[at - row + 1] if abs(at - row) <= 1 else jnp.zeros((CH, CH), f32) for at in range(RW)]
            whole = jnp.concatenate([jnp.concatenate(blocks[i : i + 4], axis=1) for i in (0, 4)], axis=1)
            rows[row * CH : (row + 1) * CH, d * FULL : (d + 1) * FULL] = whole.astype(bf16)
    turned = dot(swap, rows[...]).astype(bf16)
    for d in range(3):
        main = dot_nt(turned[:, d * FULL : (d + 1) * FULL], swap)
        b_main[:, d * FULL : (d + 1) * FULL] = main.astype(bf16)
        at = d * (FULL + EDGE)
        b_back[:, at : at + FULL] = dot_nt(same, jnp.where(inner, main, 0.0).astype(bf16)).astype(bf16)
        back_edge = jnp.zeros((FULL, EDGE), f32)
        for a in range(3):
            w = weight[a * 3 + d]
            back_edge = jnp.where(step_back == a - 1, dot_nt(dot_nt(ro, w).astype(bf16), re), back_edge)
        high = jnp.where(odd, taps_of[d][0], taps_of[d][2]).astype(bf16)
        low = jnp.where(odd, taps_of[d][2], taps_of[d][0]).astype(bf16)
        for i, j, w in ((0, 0, high), (1, 0, low), (1, 1, high), (0, 1, low)):
            b_edge[i, j, d * CH : (d + 1) * CH] = w
        b_back[:, at + FULL : at + FULL + EDGE] = back_edge.astype(bf16)

    ow = out_weight[...].astype(f32)
    line = iota((32, CH), 0)
    second = jnp.where(line < 16, div(line, 8), mod(div(line, 2), 2)) == 1
    rows_w = jnp.where(second, ow[1:2, :], ow[0:1, :]).astype(bf16)
    pr, pc = iota((16, FULL), 0), iota((16, FULL), 1)
    kept = (mod(pr, RW) == mod(pc, RW)) & (mod(pr, RW) > 0) & (mod(pr, RW) < RW - 1)
    p_main[...] = jnp.where(kept, dot_nt(rows_w[:16], ro), 0.0).astype(bf16)

    def edge_match(line, e, m):
        inside = (line < 16) & (mod(line, 8) == edge_row(e, odd))
        outer = (div(line, 4) == 4 + m) & (e == jnp.where(mod(line, 2) == 0, 0, 3))
        return inside | outer

    lr, lc = iota((32, EDGE), 0), iota((32, EDGE), 1)
    wide = dot_nt(rows_w, re)
    for m in range(2):
        both = jnp.where(edge_match(lr, div(lc, CH), m), wide, 0.0)
        for i in range(2):
            p_edge[m, i] = both[:, i * 64 : i * 64 + 64].astype(bf16)
    for k in range(2):
        columns[k] = dot_nt(ro, jnp.broadcast_to(ow[k : k + 1, :], (128, CH)).astype(bf16))
    tr, tc = iota((EDGE, 32), 0), iota((EDGE, 32), 1)
    e = div(tr, CH)
    off = (e == 0) & ((place == 0) | (place == lax.axis_size("space") - 1))
    tall = dot_nt(re, rows_w)
    for m in range(2):
        spread[m] = jnp.where(edge_match(tc, e, m) & ~off, tall, 0.0).astype(bf16)


def main_kernel(feat, skip, across, beside, b_main, b_edge, p_main, slope, part, outer, taps, pre, act):
    for m in range(2):
        x = feat[m]
        for d in range(3):
            taps[d * FULL : (d + 1) * FULL] = moved(x, d - 1)
        pre[...] = dot(b_main[...], taps[...])

        def rows(i, _):
            at = pl.ds(pl.multiple_of(i * 16, 16), 16)
            for half in range(2):
                cols = slice(half * 512, half * 512 + 512)
                a, s = gelu_pair(pre[at, cols] + skip[m, at, cols].astype(f32))
                act[at, cols] = a.astype(bf16)
                slope[m, at, cols] = s
            return 0

        lax.fori_loop(0, FULL // 16, rows, 0)
        part[m] = dot(p_main[...], act[...])
        at = m * PK
        outer[m, 0:32] = three(b_edge[0, 0], across[at : at + 32])
        outer[m, 32:64] = three(b_edge[0, 1], beside[at : at + 32])


def side(i, m, got, b_edge, p_edge, lent, outer, slope, pre, act):
    at = m * PK
    pre[0:32] = outer[m, i * 32 : i * 32 + 32] + got[at + 32 : at + 64].astype(f32)
    pre[32:64] = three(b_edge[1, i], got[at : at + 32]) + lent[m, i * 32 : i * 32 + 32]
    for step in range(4):
        near = slice(step * 16, step * 16 + 16)
        to = (step + 2 * i) % 4 * 16
        rows = slice(to, to + 16)
        for half in range(2):
            cols = slice(half * 512, half * 512 + 512)
            a, s = gelu_pair(pre[near, cols])
            act[rows, cols] = a.astype(bf16)
            slope[m, rows, cols] = s
    return dot(p_edge[m, i], act[...])


def halo_goal(h, got, rest):
    line = iota((8, W), 0)
    terms = got[2 * PK : PKT].astype(f32)
    for k in range(2):
        value = (terms[k : k + 1] + terms[2 + k : 3 + k]) + terms[4 + k : 5 + k]
        rest = jnp.where(mod(line, 4) == 2 * k + h, value, rest)
    return rest


def beside_kernel(got, b_edge, p_edge, part, lent, outer, slope, own, halo_target, pre, act):
    halo = jnp.zeros((8, W), f32)
    for m in range(2):
        more = side(1, m, got, b_edge, p_edge, lent, outer, slope, pre, act)
        own[m * 16 : m * 16 + 16] = part[m] + more[:16]
        halo = halo + more[16:24]
    own[32:40] = halo
    halo_target[...] = halo_goal(1, got, jnp.zeros((8, W), f32))


def across_kernel(got, b_edge, p_edge, lent, outer, some, some_target, slope, own, send, halo_target, pre, act):
    halo = some[32:40]
    for m in range(2):
        more = side(0, m, got, b_edge, p_edge, lent, outer, slope, pre, act)
        own[m * 16 : m * 16 + 16] = some[m * 16 : m * 16 + 16] + more[:16]
        halo = halo + more[16:24]
    own[32:40] = halo
    both = jnp.concatenate([own[:, :512], own[:, 512:]], axis=0).astype(bf16)
    for k in range(8):
        send[k] = both
    halo_target[...] = halo_goal(0, got, some_target[...])


def back_kernel(got, own, target, halo_target, slope, slope_across, slope_beside, spread, columns, b_back, out, grad, plain, ga, taps, ready, sems):
    me = lax.axis_index("member")
    width = 256
    for c in range(512 // width):
        here = [slice(h * 512 + c * width, h * 512 + (c + 1) * width) for h in range(2)]
        mine, turned, sums = [], [], []
        for h in range(2):
            o0, o1, oh = own[0:16, here[h]], own[16:32, here[h]], own[32:40, here[h]]
            t = smooth_slope(o0 - o1)
            mine.append((o0, o1, oh))
            turned.append(jnp.concatenate([oh[4:], oh[:4]], axis=0))
            sums.append([t, -t, jnp.zeros_like(oh), smooth_slope(turned[h] - oh)])
        for j in range(1, 8):
            theirs = got[mod(me + j, 8), :, c * width : (c + 1) * width].astype(f32)
            for h in range(2):
                o0, o1, oh = mine[h]
                x = theirs[40 * h : 40 * h + 40]
                x0, x1, xh = x[0:16], x[16:32], x[32:40]
                sums[h][0] += smooth_slope(o0 - x0) + smooth_slope(o0 - x1)
                sums[h][1] += smooth_slope(o1 - x0) + smooth_slope(o1 - x1)
                sums[h][2] += smooth_slope(oh - xh)
                sums[h][3] += smooth_slope(turned[h] - xh)
        for h in range(2):
            o0, o1, oh = mine[h]
            t = target[:, here[h]]
            others = sums[h][2] + jnp.concatenate([sums[h][3][4:], sums[h][3][:4]], axis=0)
            gh = smooth_slope(oh - halo_target[:, here[h]]) - others * (1.0 / 15.0)
            tail = jnp.concatenate([gh, jnp.zeros_like(gh)], axis=0).astype(bf16)
            for m, o in enumerate((o0, o1)):
                g = (smooth_slope(o - t) - sums[h][m] * (1.0 / 15.0)).astype(bf16)
                grad[m, 0:16, here[h]] = g
                plain[m, :, here[h]] = g.astype(f32)
                grad[m, 16:32, here[h]] = tail
    size = FULL + EDGE
    copies = []
    for m in range(2):
        ga[m] = dot(spread[m], grad[m])
        for h in range(2):
            cols = slice(h * 512, h * 512 + 512)
            g0, g1 = (jnp.concatenate([plain[m, k : k + 8, cols]] * 2, axis=0) for k in (0, 8))
            for i in range(FULL // 16):
                at = slice(i * 16, i * 16 + 16)
                w0, w1 = (jnp.concatenate([columns[k, at]] * 4, axis=1) for k in range(2))
                taps[m, size + i * 16 : size + i * 16 + 16, cols] = ((w0 * g0 + w1 * g1) * slope[m, at, cols]).astype(bf16)
        for i in range(EDGE // 16):
            at = FULL + i * 16
            edge = (slope_beside if i > 3 else slope_across)[m, i % 4 * 16 : i % 4 * 16 + 16]
            taps[m, size + at : size + at + 16] = (ga[m, i * 16 : i * 16 + 16] * edge).astype(bf16)
        g = taps[m, size : 2 * size]
        taps[m, 0:size] = moved(g, 1)
        taps[m, 2 * size : 3 * size] = moved(g, -1)
    for m in range(2):
        for h in range(2):
            cols = slice(h * 512, h * 512 + 512)
            ready[m, :, cols] = dot(b_back[...], taps[m, :, cols]).astype(bf16)
            copy = pltpu.make_async_copy(ready.at[m, :, cols], out.at[m, :, cols], sems.at[2 * m + h])
            copy.start()
            copies.append(copy)
    for copy in copies:
        copy.wait()


def call(kernel, outs, scratch, flops, *args, far=(), far_out=False, grant=32):
    near = pl.BlockSpec(memory_space=pltpu.VMEM)
    hbm = pl.BlockSpec(memory_space=pltpu.HBM)
    args = [pltpu.with_memory_space_constraint(x, pltpu.HBM) if i in far else x for i, x in enumerate(args)]
    return pl.pallas_call(
        kernel,
        out_shape=outs,
        in_specs=[hbm if i in far else near for i in range(len(args))],
        out_specs=[hbm if far_out else near] * len(outs),
        scratch_shapes=scratch,
        compiler_params=pltpu.CompilerParams(vmem_limit_bytes=grant * 1024 * 1024),
        cost_estimate=pl.CostEstimate(flops=flops, bytes_accessed=1 << 20, transcendentals=0),
    )(*args)


def local(features, skip, conv_weight, out_weight, target):
    S = jax.ShapeDtypeStruct
    V = pltpu.VMEM
    feat = features.reshape(2, FULL, W)
    bypass = skip.reshape(2, FULL, W)
    goal = target.reshape(16, W)
    weight = conv_weight.reshape(9, CH, CH)
    dma = pltpu.SemaphoreType.DMA
    across, beside, lent = call(
        pack_kernel,
        [S((PKT, W), bf16), S((PKT, W), bf16), S((2, 2 * CH, W), f32)],
        [
            V((2, FULL, W), bf16),
            V((2, FULL, W), bf16),
            V((16, W), f32),
            V((9, CH, CH), bf16),
            dma((6,)),
        ],
        1 << 29,
        feat,
        bypass,
        goal,
        weight,
        far=(0, 1, 2, 3),
    )
    count = lax.axis_size("space")
    got_across = lax.ppermute(across, "space", [(i, ((i + 1) ^ 1) - 1) for i in range(1, count - 1)])
    got_beside = lax.ppermute(beside, "space", [(i, i ^ 1) for i in range(count)])
    b_main, b_edge, b_back, p_main, p_edge, spread, columns = call(
        mats_kernel,
        [
            S((FULL, 3 * FULL), bf16),
            S((2, 2, 3 * CH, CH), bf16),
            S((FULL, 3 * (FULL + EDGE)), bf16),
            S((16, FULL), bf16),
            S((2, 2, 32, 2 * CH), bf16),
            S((2, EDGE, 32), bf16),
            S((2, FULL, 128), f32),
        ],
        [V((FULL, 3 * FULL), bf16)],
        1 << 31,
        weight,
        out_weight,
    )
    slope, part, outer = call(
        main_kernel,
        [S((2, FULL, W), f32), S((2, 16, W), f32), S((2, 2 * CH, W), f32)],
        [V((3 * FULL, W), bf16), V((FULL, W), f32), V((FULL, W), bf16)],
        1 << 31,
        feat,
        bypass,
        across,
        beside,
        b_main,
        b_edge,
        p_main,
    )
    slope_beside, some, some_target = call(
        beside_kernel,
        [S((2, 2 * CH, W), f32), S((40, W), f32), S((8, W), f32)],
        [V((2 * CH, W), f32), V((2 * CH, W), bf16)],
        1 << 29,
        got_beside,
        b_edge,
        p_edge,
        part,
        lent,
        outer,
    )
    slope_across, own, send, halo_target = call(
        across_kernel,
        [S((2, 2 * CH, W), f32), S((40, W), f32), S((8, 80, 512), bf16), S((8, W), f32)],
        [V((2 * CH, W), f32), V((2 * CH, W), bf16)],
        1 << 29,
        got_across,
        b_edge,
        p_edge,
        lent,
        outer,
        some,
        some_target,
    )
    got = lax.all_to_all(send, "member", split_axis=0, concat_axis=0, tiled=True)
    size = FULL + EDGE
    (out,) = call(
        back_kernel,
        [S((2, FULL, W), bf16)],
        [
            V((2, 32, W), bf16),
            V((2, 16, W), f32),
            V((2, EDGE, W), f32),
            V((2, 3 * size, W), bf16),
            V((2, FULL, W), bf16),
            dma((4,)),
        ],
        1 << 31,
        got,
        own,
        goal,
        halo_target,
        slope,
        slope_across,
        slope_beside,
        spread,
        columns,
        b_back,
        far_out=True,
    )
    return out.reshape(2, CH, RW, W)


def solution(mesh):
    placed = (
        P("member", None, "space", None),
        P("member", None, "space", None),
        P(),
        P(),
        P(None, "space", None),
    )
    return jax.shard_map(
        local,
        mesh=mesh,
        in_specs=placed,
        out_specs=P("member", None, "space", None),
        check_vma=False,
    )
```

```python
import functools
import math

import jax
import jax.numpy as jnp
from jax import lax
from jax.experimental import pallas as pl
from jax.experimental.pallas import tpu as pltpu
from jax.sharding import PartitionSpec as P

root_coef = math.sqrt(2.0 / math.pi)
cubic_coef = 0.044715
smooth = 0.25

CH = 32
RW = 8
W = 1024
FULL = CH * RW
EDGE = 4 * CH
PK = 64
PKT = 2 * PK + 8
bf16, f32 = jnp.bfloat16, jnp.float32


def iota(shape, dim):
    return lax.broadcasted_iota(jnp.int32, shape, dim)


def dot(a, b):
    return jnp.dot(a, b, preferred_element_type=f32)


def dot_nt(a, b):
    return lax.dot_general(a, b, (((1,), (1,)), ((), ())), preferred_element_type=f32)


def mod(a, n):
    return jnp.bitwise_and(a, n - 1)


def div(a, n):
    return lax.shift_right_logical(a, int(math.log2(n)))


def edge_row(e, odd):
    row = jnp.where(e < 2, e - 1, e + 5)
    return jnp.where(odd, 7 - row, row)


def facing(x):
    return jnp.bitwise_xor(x, 1)


def moved(x, step):
    zero = jnp.zeros((x.shape[0], 1), x.dtype)
    if step == 1:
        return jnp.concatenate([x[:, 1:], zero], axis=1)
    if step == -1:
        return jnp.concatenate([zero, x[:, :-1]], axis=1)
    return x


def three(matrix, x):
    y, n = dot(matrix, x), CH
    return moved(y[0:n], -1) + y[n : 2 * n] + moved(y[2 * n : 3 * n], 1)


def gelu_pair(v):
    u = v * v
    h = 0.5 + 0.5 * jnp.tanh(v * (root_coef + (root_coef * cubic_coef) * u))
    slope = h + (v * (h - h * h)) * (2.0 * root_coef + (6.0 * root_coef * cubic_coef) * u)
    return v * h, slope


def smooth_slope(u):
    return u * lax.rsqrt(u * u + smooth * smooth)


def edge_rows(odd, weight):
    r, c = iota((EDGE, FULL), 0), iota((EDGE, FULL), 1)
    q = div(r, CH)
    top = (q < 2) != odd
    row = jnp.where(top, mod(q, 2), 7 - mod(q, 2))
    pick = ((div(c, RW) == mod(r, CH)) & (mod(c, RW) == row)).astype(f32).astype(bf16)
    r2, c2 = iota((2 * CH, FULL), 0), iota((2 * CH, FULL), 1)
    row = edge_row(1 + div(r2, CH), odd)
    pick2 = ((div(c2, RW) == mod(r2, CH)) & (mod(c2, RW) == row)).astype(f32).astype(bf16)
    blocks, none = [], jnp.zeros((CH, 2 * CH), f32)
    for d in range(3):
        low, mid, high = (weight[a * 3 + d].astype(f32) for a in range(3))
        one = jnp.concatenate([mid, jnp.where(odd, low, high), none], axis=1)
        two = jnp.concatenate([none, mid, jnp.where(odd, high, low)], axis=1)
        blocks += [one, two]
    lend = dot(jnp.concatenate(blocks, axis=0).astype(bf16), pick)
    pick = pick.astype(f32)
    every = jnp.concatenate([lend, pick[0:32], pick[64:96]], axis=0).astype(bf16)

    def rows(feat, skip):
        y = dot(every, feat)
        part = (moved(y[0:64], -1) + y[64:128]) + (moved(y[128:192], 1) + dot(pick2, skip))
        return y[192:256].astype(bf16), part

    return rows


def pack_kernel(feat_in, skip_in, target_in, weight_in, one, two, lent, feat, skip, target, weight, sems):
    copies = [pltpu.make_async_copy(target_in, target, sems.at[4]), pltpu.make_async_copy(weight_in, weight, sems.at[5])]
    for m in range(2):
        copies.append(pltpu.make_async_copy(feat_in.at[m], feat.at[m], sems.at[m]))
        copies.append(pltpu.make_async_copy(skip_in.at[m], skip.at[m], sems.at[2 + m]))
    for copy in copies:
        copy.start()
    odd = mod(lax.axis_index("space"), 2) == 1
    copies[0].wait()
    copies[1].wait()
    line = iota((8, W), 0)
    for out, at, other in ((one, 0, 7), (two, 7, 0)):
        left = [jnp.where(odd, target[k + other : k + other + 1, :], target[k + at : k + at + 1, :]) for k in (0, 8)]
        total = jnp.zeros((8, W), f32)
        for term in range(3):
            for k in range(2):
                part = left[k].astype(bf16).astype(f32)
                left[k] = left[k] - part
                total = jnp.where(line == 2 * term + k, part, total)
        out[2 * PK : PKT] = total.astype(bf16)
    rows = edge_rows(odd, weight)
    for m in range(2):
        copies[2 + 2 * m].wait()
        copies[3 + 2 * m].wait()
        x, part = rows(feat[m], skip[m])
        lent[m] = part
        part = part.astype(bf16)
        one[m * PK : m * PK + 32] = x[0:32]
        two[m * PK : m * PK + 32] = x[32:64]
        one[m * PK + 32 : m * PK + 64] = part[:32]
        two[m * PK + 32 : m * PK + 64] = part[32:]


def mats_kernel(weight, out_weight, b_main, b_edge, b_back, p_main, p_edge, spread, columns, rows):
    place = lax.axis_index("space")
    odd = mod(place, 2) == 1
    ro = (div(iota((FULL, CH), 0), RW) == iota((FULL, CH), 1)).astype(f32).astype(bf16)
    re = (mod(iota((EDGE, CH), 0), CH) == iota((EDGE, CH), 1)).astype(f32).astype(bf16)
    r, c = iota((FULL, FULL), 0), iota((FULL, FULL), 1)
    swap = ((div(r, RW) == mod(c, CH)) & (mod(r, RW) == div(c, CH))).astype(f32).astype(bf16)
    same = (r == c).astype(f32).astype(bf16)
    inner = (mod(r, RW) > 0) & (mod(r, RW) < RW - 1)
    br, bc = iota((FULL, EDGE), 0), iota((FULL, EDGE), 1)
    step_back = mod(br, RW) - edge_row(div(bc, CH), odd)
    taps_of = [[weight[a * 3 + d].astype(f32) for a in range(3)] for d in range(3)]
    for d in range(3):
        taps = taps_of[d]
        for row in range(RW):
            blocks = [taps[at - row + 1] if abs(at - row) <= 1 else jnp.zeros((CH, CH), f32) for at in range(RW)]
            whole = jnp.concatenate([jnp.concatenate(blocks[i : i + 4], axis=1) for i in (0, 4)], axis=1)
            rows[row * CH : (row + 1) * CH, d * FULL : (d + 1) * FULL] = whole.astype(bf16)
    turned = dot(swap, rows[...]).astype(bf16)
    for d in range(3):
        main = dot_nt(turned[:, d * FULL : (d + 1) * FULL], swap)
        b_main[:, d * FULL : (d + 1) * FULL] = main.astype(bf16)
        at = d * (FULL + EDGE)
        b_back[:, at : at + FULL] = dot_nt(same, jnp.where(inner, main, 0.0).astype(bf16)).astype(bf16)
        back_edge = jnp.zeros((FULL, EDGE), f32)
        for a in range(3):
            w = weight[a * 3 + d]
            back_edge = jnp.where(step_back == a - 1, dot_nt(dot_nt(ro, w).astype(bf16), re), back_edge)
        high = jnp.where(odd, taps_of[d][0], taps_of[d][2]).astype(bf16)
        low = jnp.where(odd, taps_of[d][2], taps_of[d][0]).astype(bf16)
        for i, j, w in ((0, 0, high), (1, 0, low), (1, 1, high), (0, 1, low)):
            b_edge[i, j, d * CH : (d + 1) * CH] = w
        b_back[:, at + FULL : at + FULL + EDGE] = back_edge.astype(bf16)

    ow = out_weight[...].astype(f32)
    line = iota((32, CH), 0)
    second = jnp.where(line < 16, div(line, 8), mod(div(line, 2), 2)) == 1
    rows_w = jnp.where(second, ow[1:2, :], ow[0:1, :]).astype(bf16)
    pr, pc = iota((16, FULL), 0), iota((16, FULL), 1)
    kept = (mod(pr, RW) == mod(pc, RW)) & (mod(pr, RW) > 0) & (mod(pr, RW) < RW - 1)
    p_main[...] = jnp.where(kept, dot_nt(rows_w[:16], ro), 0.0).astype(bf16)

    def edge_match(line, e, m):
        inside = (line < 16) & (mod(line, 8) == edge_row(e, odd))
        outer = (div(line, 4) == 4 + m) & (e == jnp.where(mod(line, 2) == 0, 0, 3))
        return inside | outer

    lr, lc = iota((32, EDGE), 0), iota((32, EDGE), 1)
    wide = dot_nt(rows_w, re)
    for m in range(2):
        both = jnp.where(edge_match(lr, div(lc, CH), m), wide, 0.0)
        for i in range(2):
            p_edge[m, i] = both[:, i * 64 : i * 64 + 64].astype(bf16)
    for k in range(2):
        columns[k] = dot_nt(ro, jnp.broadcast_to(ow[k : k + 1, :], (128, CH)).astype(bf16))
    tr, tc = iota((EDGE, 32), 0), iota((EDGE, 32), 1)
    e = div(tr, CH)
    off = (e == 0) & ((place == 0) | (place == lax.axis_size("space") - 1))
    tall = dot_nt(re, rows_w)
    for m in range(2):
        spread[m] = jnp.where(edge_match(tc, e, m) & ~off, tall, 0.0).astype(bf16)


def main_kernel(feat, skip, across, beside, b_main, b_edge, p_main, slope, part, outer, taps, pre, act):
    for m in range(2):
        x = feat[m]
        for d in range(3):
            taps[d * FULL : (d + 1) * FULL] = moved(x, d - 1)
        pre[...] = dot(b_main[...], taps[...])

        def rows(i, _):
            at = pl.ds(pl.multiple_of(i * 16, 16), 16)
            for half in range(2):
                cols = slice(half * 512, half * 512 + 512)
                a, s = gelu_pair(pre[at, cols] + skip[m, at, cols].astype(f32))
                act[at, cols] = a.astype(bf16)
                slope[m, at, cols] = s
            return 0

        lax.fori_loop(0, FULL // 16, rows, 0)
        part[m] = dot(p_main[...], act[...])
        at = m * PK
        outer[m, 0:32] = three(b_edge[0, 0], across[at : at + 32])
        outer[m, 32:64] = three(b_edge[0, 1], beside[at : at + 32])


def side(i, m, got, b_edge, p_edge, lent, outer, slope, pre, act):
    at = m * PK
    pre[0:32] = outer[m, i * 32 : i * 32 + 32] + got[at + 32 : at + 64].astype(f32)
    pre[32:64] = three(b_edge[1, i], got[at : at + 32]) + lent[m, i * 32 : i * 32 + 32]
    for step in range(4):
        near = slice(step * 16, step * 16 + 16)
        to = (step + 2 * i) % 4 * 16
        rows = slice(to, to + 16)
        for half in range(2):
            cols = slice(half * 512, half * 512 + 512)
            a, s = gelu_pair(pre[near, cols])
            act[rows, cols] = a.astype(bf16)
            slope[m, rows, cols] = s
    return dot(p_edge[m, i], act[...])


def halo_goal(h, got, rest):
    line = iota((8, W), 0)
    terms = got[2 * PK : PKT].astype(f32)
    for k in range(2):
        value = (terms[k : k + 1] + terms[2 + k : 3 + k]) + terms[4 + k : 5 + k]
        rest = jnp.where(mod(line, 4) == 2 * k + h, value, rest)
    return rest


def beside_kernel(got, b_edge, p_edge, part, lent, outer, slope, own, halo_target, pre, act):
    halo = jnp.zeros((8, W), f32)
    for m in range(2):
        more = side(1, m, got, b_edge, p_edge, lent, outer, slope, pre, act)
        own[m * 16 : m * 16 + 16] = part[m] + more[:16]
        halo = halo + more[16:24]
    own[32:40] = halo
    halo_target[...] = halo_goal(1, got, jnp.zeros((8, W), f32))


def across_kernel(got, b_edge, p_edge, lent, outer, some, some_target, slope, own, send, halo_target, pre, act):
    halo = some[32:40]
    for m in range(2):
        more = side(0, m, got, b_edge, p_edge, lent, outer, slope, pre, act)
        own[m * 16 : m * 16 + 16] = some[m * 16 : m * 16 + 16] + more[:16]
        halo = halo + more[16:24]
    own[32:40] = halo
    both = jnp.concatenate([own[:, :512], own[:, 512:]], axis=0).astype(bf16)
    for k in range(8):
        send[k] = both
    halo_target[...] = halo_goal(0, got, some_target[...])


def back_kernel(got, own, target, halo_target, slope, slope_across, slope_beside, spread, columns, b_back, out, grad, plain, ga, taps, ready, sems):
    me = lax.axis_index("member")
    width = 512
    for c in range(512 // width):
        here = [slice(h * 512 + c * width, h * 512 + (c + 1) * width) for h in range(2)]
        mine, turned, sums = [], [], []
        for h in range(2):
            o0, o1, oh = own[0:16, here[h]], own[16:32, here[h]], own[32:40, here[h]]
            t = smooth_slope(o0 - o1)
            mine.append((o0, o1, oh))
            turned.append(jnp.concatenate([oh[4:], oh[:4]], axis=0))
            sums.append([t, -t, jnp.zeros_like(oh), smooth_slope(turned[h] - oh)])
        for j in range(1, 8):
            theirs = got[mod(me + j, 8), :, c * width : (c + 1) * width].astype(f32)
            for h in range(2):
                o0, o1, oh = mine[h]
                x = theirs[40 * h : 40 * h + 40]
                x0, x1, xh = x[0:16], x[16:32], x[32:40]
                sums[h][0] += smooth_slope(o0 - x0) + smooth_slope(o0 - x1)
                sums[h][1] += smooth_slope(o1 - x0) + smooth_slope(o1 - x1)
                sums[h][2] += smooth_slope(oh - xh)
                sums[h][3] += smooth_slope(turned[h] - xh)
        for h in range(2):
            o0, o1, oh = mine[h]
            t = target[:, here[h]]
            others = sums[h][2] + jnp.concatenate([sums[h][3][4:], sums[h][3][:4]], axis=0)
            gh = smooth_slope(oh - halo_target[:, here[h]]) - others * (1.0 / 15.0)
            tail = jnp.concatenate([gh, jnp.zeros_like(gh)], axis=0).astype(bf16)
            for m, o in enumerate((o0, o1)):
                g = (smooth_slope(o - t) - sums[h][m] * (1.0 / 15.0)).astype(bf16)
                grad[m, 0:16, here[h]] = g
                plain[m, :, here[h]] = g.astype(f32)
                grad[m, 16:32, here[h]] = tail
    size = FULL + EDGE
    copies = []
    for m in range(2):
        ga[m] = dot(spread[m], grad[m])
        for h in range(2):
            cols = slice(h * 512, h * 512 + 512)
            g0, g1 = (jnp.concatenate([plain[m, k : k + 8, cols]] * 2, axis=0) for k in (0, 8))
            for i in range(FULL // 16):
                at = slice(i * 16, i * 16 + 16)
                w0, w1 = (jnp.concatenate([columns[k, at]] * 4, axis=1) for k in range(2))
                taps[m, size + i * 16 : size + i * 16 + 16, cols] = ((w0 * g0 + w1 * g1) * slope[m, at, cols]).astype(bf16)
        for i in range(EDGE // 16):
            at = FULL + i * 16
            edge = (slope_beside if i > 3 else slope_across)[m, i % 4 * 16 : i % 4 * 16 + 16]
            taps[m, size + at : size + at + 16] = (ga[m, i * 16 : i * 16 + 16] * edge).astype(bf16)
        g = taps[m, size : 2 * size]
        taps[m, 0:size] = moved(g, 1)
        taps[m, 2 * size : 3 * size] = moved(g, -1)
    for m in range(2):
        for h in range(2):
            cols = slice(h * 512, h * 512 + 512)
            ready[m, :, cols] = dot(b_back[...], taps[m, :, cols]).astype(bf16)
            copy = pltpu.make_async_copy(ready.at[m, :, cols], out.at[m, :, cols], sems.at[2 * m + h])
            copy.start()
            copies.append(copy)
    for copy in copies:
        copy.wait()


def call(kernel, outs, scratch, flops, *args, far=(), far_out=False, grant=32):
    near = pl.BlockSpec(memory_space=pltpu.VMEM)
    hbm = pl.BlockSpec(memory_space=pltpu.HBM)
    args = [pltpu.with_memory_space_constraint(x, pltpu.HBM) if i in far else x for i, x in enumerate(args)]
    return pl.pallas_call(
        kernel,
        out_shape=outs,
        in_specs=[hbm if i in far else near for i in range(len(args))],
        out_specs=[hbm if far_out else near] * len(outs),
        scratch_shapes=scratch,
        compiler_params=pltpu.CompilerParams(vmem_limit_bytes=grant * 1024 * 1024),
        cost_estimate=pl.CostEstimate(flops=flops, bytes_accessed=1 << 20, transcendentals=0),
    )(*args)


def local(features, skip, conv_weight, out_weight, target):
    S = jax.ShapeDtypeStruct
    V = pltpu.VMEM
    feat = features.reshape(2, FULL, W)
    bypass = skip.reshape(2, FULL, W)
    goal = target.reshape(16, W)
    weight = conv_weight.reshape(9, CH, CH)
    dma = pltpu.SemaphoreType.DMA
    across, beside, lent = call(
        pack_kernel,
        [S((PKT, W), bf16), S((PKT, W), bf16), S((2, 2 * CH, W), f32)],
        [
            V((2, FULL, W), bf16),
            V((2, FULL, W), bf16),
            V((16, W), f32),
            V((9, CH, CH), bf16),
            dma((6,)),
        ],
        1 << 29,
        feat,
        bypass,
        goal,
        weight,
        far=(0, 1, 2, 3),
    )
    count = lax.axis_size("space")
    got_across = lax.ppermute(across, "space", [(i, ((i + 1) ^ 1) - 1) for i in range(1, count - 1)])
    got_beside = lax.ppermute(beside, "space", [(i, i ^ 1) for i in range(count)])
    b_main, b_edge, b_back, p_main, p_edge, spread, columns = call(
        mats_kernel,
        [
            S((FULL, 3 * FULL), bf16),
            S((2, 2, 3 * CH, CH), bf16),
            S((FULL, 3 * (FULL + EDGE)), bf16),
            S((16, FULL), bf16),
            S((2, 2, 32, 2 * CH), bf16),
            S((2, EDGE, 32), bf16),
            S((2, FULL, 128), f32),
        ],
        [V((FULL, 3 * FULL), bf16)],
        1 << 31,
        weight,
        out_weight,
    )
    slope, part, outer = call(
        main_kernel,
        [S((2, FULL, W), f32), S((2, 16, W), f32), S((2, 2 * CH, W), f32)],
        [V((3 * FULL, W), bf16), V((FULL, W), f32), V((FULL, W), bf16)],
        1 << 31,
        feat,
        bypass,
        across,
        beside,
        b_main,
        b_edge,
        p_main,
    )
    slope_beside, some, some_target = call(
        beside_kernel,
        [S((2, 2 * CH, W), f32), S((40, W), f32), S((8, W), f32)],
        [V((2 * CH, W), f32), V((2 * CH, W), bf16)],
        1 << 29,
        got_beside,
        b_edge,
        p_edge,
        part,
        lent,
        outer,
    )
    slope_across, own, send, halo_target = call(
        across_kernel,
        [S((2, 2 * CH, W), f32), S((40, W), f32), S((8, 80, 512), bf16), S((8, W), f32)],
        [V((2 * CH, W), f32), V((2 * CH, W), bf16)],
        1 << 29,
        got_across,
        b_edge,
        p_edge,
        lent,
        outer,
        some,
        some_target,
    )
    got = lax.all_to_all(send, "member", split_axis=0, concat_axis=0, tiled=True)
    size = FULL + EDGE
    (out,) = call(
        back_kernel,
        [S((2, FULL, W), bf16)],
        [
            V((2, 32, W), bf16),
            V((2, 16, W), f32),
            V((2, EDGE, W), f32),
            V((2, 3 * size, W), bf16),
            V((2, FULL, W), bf16),
            dma((4,)),
        ],
        1 << 31,
        got,
        own,
        goal,
        halo_target,
        slope,
        slope_across,
        slope_beside,
        spread,
        columns,
        b_back,
        far_out=True,
    )
    return out.reshape(2, CH, RW, W)


def solution(mesh):
    placed = (
        P("member", None, "space", None),
        P("member", None, "space", None),
        P(),
        P(),
        P(None, "space", None),
    )
    return jax.shard_map(
        local,
        mesh=mesh,
        in_specs=placed,
        out_specs=P("member", None, "space", None),
        check_vma=False,
    )
```
